32 devices in a mesh: groups: 2 (over x), wide: 16 (over z, y, core).
Axes of the slice: x: 2, y: 2, z: 4, core: 2. Of those that a mesh axis runs over, the one named last changes fastest.
Arguments:
- queries: bfloat16 [4096, 512], P(('groups', 'wide')), parts along dimension 0, may hold values from -200 to 200, as said below
- tree_kv: bfloat16 [2, 4096, 128], P(None, ('groups', 'wide')), parts along dimension 1, may hold values from -7 to 7, as said below
- kv_cache: bfloat16 [2, 512, 32, 128], P(None, ('groups', 'wide')), parts along dimension 1, may hold values from -6 to 6, as said below
- block_table: int32 [128, 4], P(('groups', 'wide')), parts along dimension 0, may hold values from 0 to 15, as said below
- cache_lengths: int32 [32, 4], P(('groups', 'wide')), parts along dimension 0, may hold values from 1 to 128, as said below
- parents: int32 [128, 32], P(('groups', 'wide')), parts along dimension 0, may hold values from -1 to 30, as said below
- w_out: bfloat16 [8192, 2048], P('wide'), may hold values from -0.375 to 0.375, as said below
- w_gate: bfloat16 [16, 2048, 768], P('wide'), may hold values from -0.125 to 0.125
- w_up: bfloat16 [16, 2048, 768], P('wide'), may hold values from -0.125 to 0.125
- w_down: bfloat16 [16, 768, 2048], P('wide'), may hold values from -0.4375 to 0.4375
- expert_ids: int32 [512, 8], P(('groups', 'wide')), parts along dimension 0, may hold values from 0 to 15, as said below
- gate_weights: float32 [512, 8], P(('groups', 'wide')), parts along dimension 0, may hold values from 0.05 to 0.5
Outputs:
- mixed: bfloat16 [512, 2048], P(('groups', 'wide')), parts along dimension 0
The draws below stay inside these ranges and needn't reach their ends.
There are 2 independent parts, one for each index of `groups`. The reference program is written for one: setup_inputs(seed, part) draws one part's arguments, and reference() takes and returns one part's arrays. A program takes and returns all parts, laid end to end along the dimension named above; an argument that names none is the same for every part. Nothing has to cross between parts.
Inputs may be any that keep to these rules, and one draw needn't show every extreme that they name: `queries`: its hidden draw may carry large entries. `tree_kv`: blocks of one group whose slices use the same key head are equal. `kv_cache`: pools of one group whose slices use the same key head are equal. `block_table`: each device's rows list every page of its pool once; blocks t * 2 + g are equal for all t. `cache_lengths`: rows t * 2 + g are equal for all t; every row holds one length 128 and one length 1. `parents`: node i of a tree has a parent before it; node 0 is the root with parent -1; blocks t * 2 + g are equal for all t. `w_out`: blocks of one head slice are equal. `expert_ids`: each row lists 8 different experts. Within the rows of one device no expert is listed by more than 10 rows; in every draw one expert is listed by exactly 10 rows of every device.
All inputs are finite; a program needn't handle non-finite values.
Results may differ from the reference program's by a relative error of at most 0.0083.
Values may be sent and summed in bfloat16 or wider, within the bound.
No kernel may reach another device: no remote copies, remote signals or barrier semaphores. Data moves between devices by JAX's collectives and lax.ppermute only.
A program may use at most 64 MiB of HBM per device.

```python
import math
import jax
import jax.numpy as jnp
from jax import lax

D_MODEL = 2048
KV_HEADS = 4
HEAD_DIM = 128
FF_EXP = 768
TOP_K = 8
EXPERTS = 16
ATT_TP = 8
QH_DEV = 4
HEAD_SLICE = 512
GROUPS = 2
TREE_ROWS = 32
GROUP_SEQS = 4
PAGE_LEN = 32
PAGES_SEQ = 4
CACHE_MAX = 128
POOL_DEV = 16
ROWS_G = 128
ROWS_DEV = 16
TOKENS = 256
MEAN_LOAD = 8
MOST_ROWS = 10
N_WIDE = 16


def device_heads():
    devices = jnp.arange(ATT_TP * GROUPS, dtype=jnp.int32)
    return (devices // GROUPS // (ATT_TP // KV_HEADS), devices % GROUPS)


def by_group(base):
    return jnp.tile(base, (ATT_TP,) + (1,) * (base.ndim - 1))


def node_keys(key):
    source = jax.random.fold_in(key, 7001)
    return jnp.clip(jax.random.normal(source, (KV_HEADS, GROUPS, ROWS_G, HEAD_DIM), jnp.float32), -6.0, 6.0)


def draw_tree_kv(key, part):
    key_rows = node_keys(key)
    value_rows = jnp.clip(jax.random.normal(jax.random.fold_in(key, 7002), (KV_HEADS, GROUPS, ROWS_G, HEAD_DIM), jnp.float32), -6.0, 6.0)
    head_ids, group_ids = device_heads()
    stacked = jnp.stack([key_rows[head_ids, group_ids], value_rows[head_ids, group_ids]])
    return stacked.reshape(2, ATT_TP * GROUPS * ROWS_G, HEAD_DIM).astype(jnp.bfloat16)


def draw_queries(key, part):
    device_count = ATT_TP * GROUPS
    drawn = jnp.clip(jax.random.normal(jax.random.fold_in(key, 7003), (device_count, GROUP_SEQS, TREE_ROWS, HEAD_SLICE), jnp.float32), -6.0, 6.0)
    return drawn.reshape(device_count * ROWS_G, HEAD_SLICE).astype(jnp.bfloat16)


def draw_kv_cache(key, part):
    base = jnp.clip(jax.random.normal(jax.random.fold_in(key, 7009), (2, KV_HEADS, GROUPS, POOL_DEV, PAGE_LEN, HEAD_DIM), jnp.float32), -6.0, 6.0)
    head_ids, group_ids = device_heads()
    spread = base[:, head_ids, group_ids]
    return spread.reshape(2, ATT_TP * GROUPS * POOL_DEV, PAGE_LEN, HEAD_DIM).astype(jnp.bfloat16)


def draw_block_table(key, part):
    group_keys = jax.random.split(jax.random.fold_in(key, 7005), GROUPS)
    orders = jax.vmap(lambda single: jax.random.permutation(single, POOL_DEV))(group_keys)
    tables = by_group(orders.reshape(GROUPS, GROUP_SEQS, PAGES_SEQ))
    return tables.reshape(ATT_TP * GROUPS * GROUP_SEQS, PAGES_SEQ).astype(jnp.int32)


def draw_cache_lengths(key, part):
    lengths = jax.random.randint(jax.random.fold_in(key, 7010), (GROUPS, GROUP_SEQS), 1, CACHE_MAX + 1, dtype=jnp.int32)
    longest = jax.random.randint(jax.random.fold_in(key, 7011), (GROUPS, 1), 0, GROUP_SEQS, dtype=jnp.int32)
    shortest = (longest + 1) % GROUP_SEQS
    seq_ids = jnp.arange(GROUP_SEQS, dtype=jnp.int32)[None, :]
    lengths = jnp.where(seq_ids == longest, CACHE_MAX, lengths)
    lengths = jnp.where(seq_ids == shortest, 1, lengths)
    return by_group(lengths).astype(jnp.int32)


def draw_parents(key, part):
    node_ids = jnp.arange(TREE_ROWS, dtype=jnp.int32)
    ceiling = jnp.broadcast_to(jnp.maximum(node_ids, 1), (GROUPS, GROUP_SEQS, TREE_ROWS))
    picked = jax.random.randint(jax.random.fold_in(key, 7006), (GROUPS, GROUP_SEQS, TREE_ROWS), 0, ceiling, dtype=jnp.int32)
    picked = jnp.where(node_ids == 0, -1, picked)
    return by_group(picked).reshape(ATT_TP * GROUPS * GROUP_SEQS, TREE_ROWS).astype(jnp.int32)


def draw_w_out(key, part):
    base = jnp.clip(jax.random.normal(jax.random.fold_in(key, 7012), (ATT_TP, HEAD_SLICE, D_MODEL), jnp.float32), -6.0, 6.0) * 256.0 ** (-0.5)
    slice_ids = jnp.arange(ATT_TP * GROUPS, dtype=jnp.int32) // GROUPS
    return base[slice_ids].reshape(ATT_TP * GROUPS * HEAD_SLICE, D_MODEL).astype(jnp.bfloat16)


def route_block(single, favored):
    spread = MOST_ROWS - MEAN_LOAD
    ranked = jax.random.permutation(jax.random.fold_in(single, 1), EXPERTS).astype(jnp.int32)
    ranked = jnp.where(ranked == favored, ranked[0], ranked).at[0].set(favored)
    offsets = jax.random.randint(jax.random.fold_in(single, 2), (EXPERTS // 2,), 0, spread + 1, dtype=jnp.int32)
    offsets = offsets.at[0].set(spread)
    quotas = jnp.stack([MEAN_LOAD + offsets, MEAN_LOAD - offsets], axis=1).reshape(EXPERTS)
    boundary = jnp.cumsum(quotas)
    ticket = jnp.arange(ROWS_DEV * TOP_K, dtype=jnp.int32)
    position = jnp.sum((ticket[:, None] >= boundary[None, :]).astype(jnp.int32), axis=1)
    layout = ranked[position].reshape(TOP_K, ROWS_DEV).T
    row_order = jax.random.permutation(jax.random.fold_in(single, 3), ROWS_DEV)
    layout = layout[row_order]
    rotation = jax.random.randint(jax.random.fold_in(single, 4), (ROWS_DEV, 1), 0, TOP_K, dtype=jnp.int32)
    columns = (jnp.arange(TOP_K, dtype=jnp.int32)[None, :] + rotation) % TOP_K
    return jnp.take_along_axis(layout, columns, axis=1)


def draw_expert_ids(key, part):
    device_count = TOKENS // ROWS_DEV
    favored = jax.random.randint(jax.random.fold_in(key, 7007), (), 0, EXPERTS, dtype=jnp.int32)
    device_keys = jax.random.split(jax.random.fold_in(key, 7008), device_count)
    layouts = jax.vmap(lambda single: route_block(single, favored))(device_keys)
    return layouts.reshape(TOKENS, TOP_K).astype(jnp.int32)


def block_scale(stream_key, dims, pieces, low, high):
    def one(dim, parts):
        steps = jax.random.uniform(jax.random.fold_in(jax.random.fold_in(stream_key, 6), dim), (parts,), jnp.float32, low / len(pieces), high / len(pieces))
        return jnp.repeat(jnp.exp(steps), dims[dim] // parts).reshape((-1,) + (1,) * (len(dims) - dim - 1))

    loudness = one(*pieces[0])
    for cut in pieces[1:]:
        loudness = loudness * one(*cut)
    return loudness


def normal_values(rng, dims, deviation, most, cuts=(), held_as=jnp.bfloat16):
    factor_of = block_scale(rng, dims, cuts, -0.22, 0.18) if cuts else 1.0
    entries = jax.random.normal(rng, dims, jnp.float32) * deviation * factor_of
    return jnp.minimum(jnp.maximum(entries, -most), most).astype(held_as)


def setup_inputs(seed: int = 0, part: int = 0) -> dict:
    key_of = jax.random.split(jax.random.key(seed), 13)
    part_keys = jax.random.split(jax.random.fold_in(key_of[12], part), 13)
    queries = draw_queries(jax.random.fold_in(jax.random.fold_in(key_of[12], part), 71), part)
    tree_kv = draw_tree_kv(jax.random.fold_in(jax.random.fold_in(key_of[12], part), 71), part)
    kv_cache = draw_kv_cache(jax.random.fold_in(jax.random.fold_in(key_of[12], part), 71), part)
    block_table = draw_block_table(jax.random.fold_in(jax.random.fold_in(key_of[12], part), 71), part)
    cache_lengths = draw_cache_lengths(jax.random.fold_in(jax.random.fold_in(key_of[12], part), 71), part)
    parents = draw_parents(jax.random.fold_in(jax.random.fold_in(key_of[12], part), 71), part)
    w_out = draw_w_out(jax.random.fold_in(key_of[12], 71), part)
    w_gate = normal_values(key_of[7], (EXPERTS, D_MODEL, FF_EXP), D_MODEL ** -0.5, 0.125, ((0, 16),))
    w_up = normal_values(key_of[8], (EXPERTS, D_MODEL, FF_EXP), D_MODEL ** -0.5, 0.125, ((0, 16),))
    w_down = normal_values(key_of[9], (EXPERTS, FF_EXP, D_MODEL), 192 ** -0.5, 0.4375, ((0, 16),))
    expert_ids = draw_expert_ids(jax.random.fold_in(jax.random.fold_in(key_of[12], part), 71), part)
    gate_weights = jnp.clip(jnp.exp(math.log(0.5) - 2.3025851 * jax.random.uniform(part_keys[11], (TOKENS, TOP_K), jnp.float32) ** block_scale(part_keys[11], (TOKENS, TOP_K), ((0, 16),), -0.2, 0.2)), 0.05, 0.5)
    return dict(queries=queries, tree_kv=tree_kv, kv_cache=kv_cache, block_table=block_table, cache_lengths=cache_lengths, parents=parents, w_out=w_out, w_gate=w_gate, w_up=w_up, w_down=w_down, expert_ids=expert_ids, gate_weights=gate_weights)


def ancestor_mask(parents):
    node_ids = jnp.broadcast_to(jnp.arange(TREE_ROWS, dtype=jnp.int32), parents.shape)
    columns = jnp.arange(TREE_ROWS, dtype=jnp.int32)
    reached = node_ids[:, :, None] == columns
    for repeat in range(TREE_ROWS):
        safe_ids = jnp.maximum(node_ids, 0).astype(jnp.int32)
        parent_of = jnp.take_along_axis(parents, safe_ids, axis=1).astype(jnp.int32)
        node_ids = jnp.where(node_ids >= 0, parent_of, -1).astype(jnp.int32)
        reached = reached | (node_ids[:, :, None] == columns)
    return reached


def attend_sequences(query_rows, own_keys, own_values, cache_keys, cache_values, lengths, parents):
    seq_count = parents.shape[0]
    cached = cache_keys.shape[1]
    query_heads = query_rows.reshape(seq_count, TREE_ROWS, QH_DEV, HEAD_DIM).astype(jnp.float32)
    key_rows = jnp.concatenate([cache_keys, own_keys], axis=1).astype(jnp.float32)
    value_rows = jnp.concatenate([cache_values, own_values], axis=1).astype(jnp.float32)
    scores = jnp.einsum('sqhd,skd->sqhk', query_heads, key_rows, precision=lax.Precision.HIGHEST) * (HEAD_DIM ** -0.5)
    positions = jnp.arange(cached, dtype=jnp.int32)
    cache_open = jnp.broadcast_to(positions[None, None, :] < lengths[:, None, None], (seq_count, TREE_ROWS, cached))
    allowed = jnp.concatenate([cache_open, ancestor_mask(parents)], axis=2)[:, :, None, :]
    masked = jnp.where(allowed, scores, -jnp.inf)
    highest = jnp.max(masked, axis=-1, keepdims=True)
    weights = jnp.exp(masked - highest)
    denominator = jnp.sum(weights, axis=-1, keepdims=True)
    rounded = lax.optimization_barrier(weights.astype(jnp.bfloat16)).astype(jnp.float32)
    blended = jnp.einsum('sqhk,skd->sqhd', rounded, value_rows, precision=lax.Precision.HIGHEST)
    return (blended / denominator).reshape(seq_count * TREE_ROWS, QH_DEV * HEAD_DIM).astype(jnp.bfloat16)


def reference(queries, tree_kv, kv_cache, block_table, cache_lengths, parents, w_out, w_gate, w_up, w_down, expert_ids, gate_weights):
    key_pool = kv_cache[0]
    value_pool = kv_cache[1]

    def one_device(summed, device):
        first_row = (device * ROWS_G).astype(jnp.int32)
        first_seq = (device * GROUP_SEQS).astype(jnp.int32)
        query_rows = lax.dynamic_slice_in_dim(queries, first_row, ROWS_G, 0)
        own_keys = lax.dynamic_slice_in_dim(tree_kv[0], first_row, ROWS_G, 0).reshape(GROUP_SEQS, TREE_ROWS, HEAD_DIM)
        own_values = lax.dynamic_slice_in_dim(tree_kv[1], first_row, ROWS_G, 0).reshape(GROUP_SEQS, TREE_ROWS, HEAD_DIM)
        pages = (lax.dynamic_slice_in_dim(block_table, first_seq, GROUP_SEQS, 0) + device * POOL_DEV).astype(jnp.int32)
        cache_keys = key_pool[pages].reshape(GROUP_SEQS, CACHE_MAX, HEAD_DIM)
        cache_values = value_pool[pages].reshape(GROUP_SEQS, CACHE_MAX, HEAD_DIM)
        lengths = lax.dynamic_slice_in_dim(cache_lengths, device.astype(jnp.int32), 1, 0).reshape(GROUP_SEQS)
        local_parents = lax.dynamic_slice_in_dim(parents, first_seq, GROUP_SEQS, 0)
        slice_rows = lax.dynamic_slice_in_dim(w_out, (device * HEAD_SLICE).astype(jnp.int32), HEAD_SLICE, 0)
        attended = attend_sequences(query_rows, own_keys, own_values, cache_keys, cache_values, lengths, local_parents)
        projected = jnp.dot(attended, slice_rows, preferred_element_type=jnp.float32)
        group_slot = (device % GROUPS).astype(jnp.int32)
        return summed.at[group_slot].add(projected), None

    initial = jnp.zeros((GROUPS, ROWS_G, D_MODEL), jnp.float32)
    summed, unused = lax.scan(one_device, initial, jnp.arange(N_WIDE, dtype=jnp.int32))
    hidden = summed.astype(jnp.bfloat16).reshape(GROUPS, ATT_TP, ROWS_DEV, D_MODEL)
    hidden = jnp.transpose(hidden, (1, 0, 2, 3)).reshape(TOKENS, D_MODEL)

    capacity = N_WIDE * MOST_ROWS
    row_numbers = jnp.arange(TOKENS, dtype=jnp.int32)

    def expert_step(running, packed):
        number, gate_matrix, up_matrix, down_matrix = packed
        matches = expert_ids == number
        chosen = jnp.any(matches, axis=1)
        row_weight = jnp.sum(jnp.where(matches, gate_weights, 0.0), axis=1)
        ranking = jnp.cumsum(chosen.astype(jnp.int32)) - 1
        target = jnp.where(chosen, ranking, capacity).astype(jnp.int32)
        picked = jnp.zeros((capacity,), jnp.int32).at[target].set(row_numbers, mode='drop')
        occupied = jnp.zeros((capacity,), jnp.float32).at[target].set(1.0, mode='drop')
        inputs = hidden[picked]
        gate_part = jnp.dot(inputs, gate_matrix, preferred_element_type=jnp.float32)
        up_part = jnp.dot(inputs, up_matrix, preferred_element_type=jnp.float32)
        activated = (jax.nn.silu(gate_part) * up_part).astype(jnp.bfloat16)
        produced = jnp.dot(activated, down_matrix, preferred_element_type=jnp.float32).astype(jnp.bfloat16)
        scaled = produced.astype(jnp.float32) * (row_weight[picked] * occupied)[:, None]
        return running.at[picked].add(scaled), None

    initial_rows = jnp.zeros((TOKENS, D_MODEL), jnp.float32)
    combined, unused_rows = lax.scan(expert_step, initial_rows, (jnp.arange(EXPERTS, dtype=jnp.int32), w_gate, w_up, w_down))
    return combined.astype(jnp.bfloat16)
```

```python
import functools

import jax
import jax.numpy as jnp
from jax import lax
from jax.experimental import pallas as pl
from jax.experimental.pallas import tpu as pltpu
from jax.sharding import PartitionSpec as P

ATT_TP = 8
CHUNKS = 2
LANES = 128


def bits_of(count):
    return count.bit_length() - 1


def exchange(block, masks):
    count = lax.axis_size("wide")
    return lax.ppermute(block, "wide", [(i, i ^ masks[i & 1]) for i in range(count)])


def slice_orders(axis_width):
    groups = axis_width // ATT_TP
    first = [groups << step for step in range(bits_of(ATT_TP))]
    second = [first[1], first[0]] + first[2:] if groups > 1 and len(first) > 2 else first
    return first, second


def relative_masks(order):
    steps = len(order)
    masks = []
    for j in range(1 << steps):
        mask = 0
        for step in range(steps):
            if j >> (steps - 1 - step) & 1:
                mask ^= order[step]
        masks.append(mask)
    return masks


def attend_kernel(
    axis_width,
    table,
    lengths,
    queries,
    tree_kv,
    kv_cache,
    parents,
    expert_ids,
    gate_weights,
    w_out,
    *refs,
):
    outs, (extra, attended, weights_in, weights_sem) = refs[:-4], refs[-4:]
    copy = pltpu.make_async_copy(w_out, weights_in, weights_sem)
    copy.start()
    seq_count, node_count = parents.shape
    head_dim = tree_kv.shape[-1]
    head_count = queries.shape[1] // head_dim
    pages = table.shape[1]
    cached = pages * kv_cache.shape[2]
    all_nodes = seq_count * node_count
    query_count = head_count * node_count
    f32, bf16 = jnp.float32, jnp.bfloat16

    shifted = [
        jnp.where(parents[s : s + 1, :] >= 0, parents[s : s + 1, :] + s * node_count, -1)
        for s in range(seq_count)
    ]
    parent_row = jnp.concatenate(shifted, axis=1)
    rows = lax.broadcasted_iota(jnp.int32, (all_nodes, all_nodes), 0)
    columns = lax.broadcasted_iota(jnp.int32, (all_nodes, all_nodes), 1)
    reached = ((rows == columns) | (rows == parent_row)).astype(f32).astype(bf16)
    for repeat in range(max(node_count - 1, 1).bit_length()):
        squared = jnp.dot(reached, reached, preferred_element_type=f32)
        reached = jnp.minimum(squared, 1.0).astype(bf16)

    node_rows = lax.broadcasted_iota(jnp.int32, (all_nodes, query_count), 0)
    query_nodes = lax.broadcasted_iota(jnp.int32, (all_nodes, query_count), 1) % node_count
    positions = lax.broadcasted_iota(jnp.int32, (cached, query_count), 0)
    for s in range(seq_count):
        own = slice(s * node_count, (s + 1) * node_count)
        spread = (node_rows == query_nodes + s * node_count).astype(f32).astype(bf16)
        tree_open = jnp.dot(reached[own], spread, preferred_element_type=f32) > 0.5
        keys = [kv_cache[0, table[s, p]] for p in range(pages)]
        values = [kv_cache[1, table[s, p]] for p in range(pages)]
        key_rows = jnp.concatenate(keys + [tree_kv[0, own]], axis=0)
        value_rows = jnp.concatenate(values + [tree_kv[1, own]], axis=0)
        query_rows = jnp.concatenate(
            [queries[own, h * head_dim : (h + 1) * head_dim] for h in range(head_count)], axis=0
        )
        scores = lax.dot_general(
            key_rows, query_rows, (((1,), (1,)), ((), ())), preferred_element_type=f32
        ) * head_dim ** (-0.5)
        cache_scores = jnp.where(positions < lengths[0, s], scores[:cached], -jnp.inf)
        tree_scores = jnp.where(tree_open, scores[cached:], -jnp.inf)
        masked = jnp.concatenate([cache_scores, tree_scores], axis=0)
        highest = jnp.max(masked, axis=0, keepdims=True)
        probs = jnp.exp(masked - highest)
        total = jnp.broadcast_to(jnp.sum(probs, axis=0, keepdims=True), (head_dim, query_count))
        blended = lax.dot_general(
            probs.astype(bf16), value_rows, (((0,), (0,)), ((), ())), preferred_element_type=f32
        )
        blended = (blended / total.T).astype(bf16)
        for h in range(head_count):
            attended[own, h * head_dim : (h + 1) * head_dim] = blended[
                h * node_count : (h + 1) * node_count
            ]

    row_count, listed = expert_ids.shape
    lane = lax.broadcasted_iota(jnp.int32, (row_count, extra.shape[1]), 1)
    weight = jnp.zeros((row_count, extra.shape[1]), f32)
    for k in range(listed):
        weight += jnp.where(
            expert_ids[:, k : k + 1] == lane % axis_width, gate_weights[:, k : k + 1], 0.0
        )
    upper = weight.astype(bf16).astype(f32)
    parts = jnp.where(lane < axis_width, upper, jnp.where(lane < 2 * axis_width, weight - upper, 0.0))
    extra[:row_count] = parts.astype(bf16)
    extra[row_count:] = jnp.zeros((row_count, extra.shape[1]), bf16)

    device = lax.axis_index("wide")
    groups = axis_width // ATT_TP
    first, second = [relative_masks(order) for order in slice_orders(axis_width)]
    block = all_nodes // ATT_TP
    picked = []
    for one, other in zip(first, second):
        target = (device ^ jnp.where(device & 1 == 0, one, other)) // groups
        picked.append(attended[pl.ds(pl.multiple_of(target * block, block), block), :])
    ordered = jnp.concatenate(picked, axis=0)
    copy.wait()
    half = all_nodes // 2
    width = outs[0].shape[1]
    for c in range(len(outs) // 2):
        projected = jnp.dot(
            ordered, weights_in[:, c * width : (c + 1) * width], preferred_element_type=f32
        )
        outs[2 * c][...] = projected[:half]
        outs[2 * c + 1][...] = projected[half:].astype(bf16)


def attend(queries, tree_kv, kv_cache, table, lengths, parents, w_out, expert_ids, gate_weights):
    axis_width = lax.axis_size("wide")
    features = w_out.shape[1]
    rows = queries.shape[0]
    own_rows = expert_ids.shape[0]
    extra_width = -(-2 * axis_width // LANES) * LANES
    smem = pl.BlockSpec(memory_space=pltpu.SMEM)
    vmem = pl.BlockSpec(memory_space=pltpu.VMEM)
    half = (rows // 2, features // CHUNKS)
    kept, sent = jax.ShapeDtypeStruct(half, jnp.float32), jax.ShapeDtypeStruct(half, jnp.bfloat16)
    return pl.pallas_call(
        functools.partial(attend_kernel, axis_width),
        out_shape=[kept, sent] * CHUNKS
        + [jax.ShapeDtypeStruct((2 * own_rows, extra_width), jnp.bfloat16)],
        in_specs=[smem, smem] + [vmem] * 6 + [pl.BlockSpec(memory_space=pl.ANY)],
        out_specs=[vmem] * (2 * CHUNKS + 1),
        scratch_shapes=[
            pltpu.VMEM(queries.shape, jnp.bfloat16),
            pltpu.VMEM(w_out.shape, jnp.bfloat16),
            pltpu.SemaphoreType.DMA,
        ],
        compiler_params=pltpu.CompilerParams(vmem_limit_bytes=16 * 1024 * 1024),
        name="attend",
    )(table, lengths, queries, tree_kv, kv_cache, parents, expert_ids, gate_weights, w_out)


def experts_kernel(axis_width, tile, *refs):
    hidden, (w_gate, w_up, w_down) = refs[:CHUNKS], refs[CHUNKS : CHUNKS + 3]
    outs, activated = refs[CHUNKS + 3 : -1], refs[-1]
    f32, bf16 = jnp.float32, jnp.bfloat16
    width = outs[0].shape[1]
    device = lax.axis_index("wide")
    parts = hidden[-1][:, width:]
    lane = lax.broadcasted_iota(jnp.int32, parts.shape, 1)
    mine = (lane == device) | (lane == device + axis_width)
    weight = jnp.sum(jnp.where(mine, parts.astype(f32), 0.0), axis=1, keepdims=True)
    hidden_width = activated.shape[1]
    half = activated.shape[0] // 2
    for n in range(hidden_width // tile):
        cut = slice(n * tile, (n + 1) * tile)
        gate_part = up_part = 0.0
        for c in range(CHUNKS):
            rows = hidden[c][:, :width]
            down = slice(c * width, (c + 1) * width)
            gate_part += jnp.dot(rows, w_gate[0, down, cut], preferred_element_type=f32)
            up_part += jnp.dot(rows, w_up[0, down, cut], preferred_element_type=f32)
        activated[:, cut] = (gate_part / (1.0 + jnp.exp(-gate_part)) * up_part).astype(bf16)
    for c in range(CHUNKS):
        for n in range(width // tile):
            cut = slice(c * width + n * tile, c * width + (n + 1) * tile)
            produced = jnp.dot(activated[...], w_down[0, :, cut], preferred_element_type=f32)
            weighted = produced * weight
            outs[2 * c][:, n * tile : (n + 1) * tile] = weighted[:half]
            outs[2 * c + 1][:, n * tile : (n + 1) * tile] = weighted[half:].astype(bf16)


def experts(hidden, w_gate, w_up, w_down):
    axis_width = lax.axis_size("wide")
    rows = hidden[0].shape[0]
    hidden_width, features = w_down.shape[1:]
    vmem = pl.BlockSpec(memory_space=pltpu.VMEM)
    tile = 256 if hidden_width % 256 == 0 else LANES
    half = (rows // 2, features // CHUNKS)
    kept, sent = jax.ShapeDtypeStruct(half, jnp.float32), jax.ShapeDtypeStruct(half, jnp.bfloat16)
    return pl.pallas_call(
        functools.partial(experts_kernel, axis_width, tile),
        out_shape=[kept, sent] * CHUNKS,
        in_specs=[vmem] * (CHUNKS + 3),
        out_specs=[vmem] * (2 * CHUNKS),
        scratch_shapes=[pltpu.VMEM((rows, hidden_width), jnp.bfloat16)],
        compiler_params=pltpu.CompilerParams(vmem_limit_bytes=48 * 1024 * 1024),
        name="experts",
    )(*hidden, w_gate, w_up, w_down)


def halved(block):
    half = block.shape[0] // 2
    return block[:half], block[half:].astype(jnp.bfloat16)


def body(
    queries,
    tree_kv,
    kv_cache,
    block_table,
    cache_lengths,
    parents,
    w_out,
    w_gate,
    w_up,
    w_down,
    expert_ids,
    gate_weights,
):
    axis_width = lax.axis_size("wide")
    steps = list(zip(*slice_orders(axis_width)))
    group_steps = [(1 << k, 1 << k) for k in range(bits_of(axis_width // ATT_TP))]
    *halves, extra = attend(
        queries, tree_kv, kv_cache, block_table, cache_lengths, parents, w_out,
        expert_ids, gate_weights,
    )
    hidden = []
    for c in range(CHUNKS):
        kept, sent = halves[2 * c], halves[2 * c + 1]
        for number, masks in enumerate(steps[:-1]):
            kept = kept + exchange(sent, masks).astype(jnp.float32)
            if number < len(steps) - 2:
                kept, sent = halved(kept)
        if c == CHUNKS - 1:
            kept = jnp.concatenate([kept, extra.astype(jnp.float32)], axis=1)
        half = kept.shape[0] // 2
        other = exchange(kept.astype(jnp.bfloat16), steps[-1]).astype(jnp.float32)
        block = kept + jnp.concatenate([other[half:], other[:half]], axis=0)
        block = block.astype(jnp.bfloat16)
        for masks in steps[-2::-1] + group_steps:
            block = jnp.concatenate([block, exchange(block, masks)], axis=0)
        hidden.append(block)
    produced = experts(hidden, w_gate, w_up, w_down)
    results = []
    for c in range(CHUNKS):
        kept, sent = produced[2 * c], produced[2 * c + 1]
        last = len(group_steps) + len(steps) - 1
        for number, masks in enumerate(group_steps[::-1] + steps):
            kept = kept + exchange(sent, masks).astype(jnp.float32)
            if number < last:
                kept, sent = halved(kept)
        results.append(kept.astype(jnp.bfloat16))
    return jnp.concatenate(results, axis=1)


def solution(mesh):
    placed = (
        P(("groups", "wide"), None),
        P(None, ("groups", "wide"), None),
        P(None, ("groups", "wide"), None, None),
        P(("groups", "wide"), None),
        P(("groups", "wide"), None),
        P(("groups", "wide"), None),
        P("wide", None),
        P("wide", None, None),
        P("wide", None, None),
        P("wide", None, None),
        P(("groups", "wide"), None),
        P(("groups", "wide"), None),
    )
    return jax.shard_map(
        body, mesh=mesh, in_specs=placed, out_specs=P(("groups", "wide"), None), check_vma=False
    )
```

```python
import functools

import jax
import jax.numpy as jnp
from jax import lax
from jax.experimental import pallas as pl
from jax.experimental.pallas import tpu as pltpu
from jax.sharding import PartitionSpec as P

ATT_TP = 8
PIECES = (8, 8)
CHUNKS = len(PIECES)
LANES = 128


def bits_of(count):
    return count.bit_length() - 1


def column_cuts(features):
    ends = [features * sum(PIECES[: c + 1]) // sum(PIECES) for c in range(CHUNKS)]
    return list(zip([0] + ends[:-1], ends))


def exchange(block, masks):
    count = lax.axis_size("wide")
    return lax.ppermute(block, "wide", [(i, i ^ masks[i & 1]) for i in range(count)])


def slice_orders(axis_width):
    groups = axis_width // ATT_TP
    first = [groups << step for step in range(bits_of(ATT_TP))]
    second = [first[1], first[0]] + first[2:] if groups > 1 and len(first) > 2 else first
    return first, second


def relative_masks(order):
    steps = len(order)
    masks = []
    for j in range(1 << steps):
        mask = 0
        for step in range(steps):
            if j >> (steps - 1 - step) & 1:
                mask ^= order[step]
        masks.append(mask)
    return masks


def attend_kernel(axis_width, *refs):
    sources, outs, scratch = refs[:9], refs[9 : 10 + 2 * CHUNKS], refs[10 + 2 * CHUNKS :]
    *inputs, attended, sems = scratch
    copies = [
        pltpu.make_async_copy(source, target, sems.at[n])
        for n, (source, target) in enumerate(zip(sources, inputs))
    ]
    for copy in copies:
        copy.start()
    for copy in copies[:-1]:
        copy.wait()
    table, lengths, parents, expert_ids, gate_weights = inputs[:5]
    queries, tree_kv, kv_cache, weights_in = inputs[5:]
    *outs, extra = outs
    seq_count, node_count = parents.shape
    head_dim = tree_kv.shape[-1]
    head_count = queries.shape[1] // head_dim
    pages = table.shape[1]
    cached = pages * kv_cache.shape[2]
    all_nodes = seq_count * node_count
    query_count = head_count * node_count
    f32, bf16 = jnp.float32, jnp.bfloat16

    shifted = [
        jnp.where(parents[s : s + 1, :] >= 0, parents[s : s + 1, :] + s * node_count, -1)
        for s in range(seq_count)
    ]
    parent_row = jnp.concatenate(shifted, axis=1)
    rows = lax.broadcasted_iota(jnp.int32, (all_nodes, all_nodes), 0)
    columns = lax.broadcasted_iota(jnp.int32, (all_nodes, all_nodes), 1)
    reached = ((rows == columns) | (rows == parent_row)).astype(f32).astype(bf16)
    for repeat in range(max(node_count - 1, 1).bit_length()):
        squared = jnp.dot(reached, reached, preferred_element_type=f32)
        reached = jnp.minimum(squared, 1.0).astype(bf16)

    node_rows = lax.broadcasted_iota(jnp.int32, (all_nodes, query_count), 0)
    query_nodes = lax.broadcasted_iota(jnp.int32, (all_nodes, query_count), 1) % node_count
    positions = lax.broadcasted_iota(jnp.int32, (cached, query_count), 0)
    for s in range(seq_count):
        own = slice(s * node_count, (s + 1) * node_count)
        spread = (node_rows == query_nodes + s * node_count).astype(f32).astype(bf16)
        tree_open = jnp.dot(reached[own], spread, preferred_element_type=f32) > 0.5
        keys = [kv_cache[0, table[s, p]] for p in range(pages)]
        values = [kv_cache[1, table[s, p]] for p in range(pages)]
        key_rows = jnp.concatenate(keys + [tree_kv[0, own]], axis=0)
        value_rows = jnp.concatenate(values + [tree_kv[1, own]], axis=0)
        query_rows = jnp.concatenate(
            [queries[own, h * head_dim : (h + 1) * head_dim] for h in range(head_count)], axis=0
        )
        scores = lax.dot_general(
            key_rows, query_rows, (((1,), (1,)), ((), ())), preferred_element_type=f32
        ) * head_dim ** (-0.5)
        cache_scores = jnp.where(positions < lengths[0, s], scores[:cached], -jnp.inf)
        tree_scores = jnp.where(tree_open, scores[cached:], -jnp.inf)
        masked = jnp.concatenate([cache_scores, tree_scores], axis=0)
        highest = jnp.max(masked, axis=0, keepdims=True)
        probs = jnp.exp(masked - highest)
        total = jnp.broadcast_to(jnp.sum(probs, axis=0, keepdims=True), (head_dim, query_count))
        blended = lax.dot_general(
            probs.astype(bf16), value_rows, (((0,), (0,)), ((), ())), preferred_element_type=f32
        )
        blended = (blended / total.T).astype(bf16)
        for h in range(head_count):
            attended[own, h * head_dim : (h + 1) * head_dim] = blended[
                h * node_count : (h + 1) * node_count
            ]

    listed, row_count = expert_ids.shape
    spread_width = extra.shape[1]
    expert = lax.broadcasted_iota(jnp.int32, (spread_width, row_count), 0)
    weight = jnp.zeros((spread_width, row_count), f32)
    for k in range(listed):
        weight += jnp.where(
            expert_ids[k : k + 1, :] == expert % axis_width, gate_weights[k : k + 1, :], 0.0
        )
    upper = weight.astype(bf16).astype(f32)
    parts = jnp.where(
        expert < axis_width, upper, jnp.where(expert < 2 * axis_width, weight - upper, 0.0)
    )
    extra[:row_count] = parts.T.astype(bf16)
    extra[row_count:] = jnp.zeros((row_count, spread_width), bf16)

    device = lax.axis_index("wide")
    groups = axis_width // ATT_TP
    first, second = [relative_masks(order) for order in slice_orders(axis_width)]
    block = all_nodes // ATT_TP
    picked = []
    for one, other in zip(first, second):
        target = (device ^ jnp.where(device & 1 == 0, one, other)) // groups
        picked.append(attended[pl.ds(pl.multiple_of(target * block, block), block), :])
    ordered = jnp.concatenate(picked, axis=0)
    copies[-1].wait()
    half = all_nodes // 2
    for c, (low, high) in enumerate(column_cuts(weights_in.shape[1])):
        projected = jnp.dot(ordered, weights_in[:, low:high], preferred_element_type=f32)
        outs[2 * c][...] = projected[:half]
        outs[2 * c + 1][...] = projected[half:].astype(bf16)


def kept_and_sent(rows, cuts):
    shapes = []
    for low, high in cuts:
        shapes.append(pltpu.VMEM((rows // 2, high - low), jnp.float32))
        shapes.append(pltpu.VMEM((rows // 2, high - low), jnp.bfloat16))
    return shapes


def attend(queries, tree_kv, kv_cache, table, lengths, parents, w_out, expert_ids, gate_weights):
    axis_width = lax.axis_size("wide")
    features = w_out.shape[1]
    rows = queries.shape[0]
    own_rows = expert_ids.shape[0]
    extra_width = -(-2 * axis_width // LANES) * LANES
    halves = kept_and_sent(rows, column_cuts(features))
    given = [table, lengths, parents, expert_ids.T, gate_weights.T, queries, tree_kv, kv_cache, w_out]
    spaces = [pltpu.SMEM] * 2 + [pltpu.VMEM] * (len(given) - 2)
    given = [pltpu.with_memory_space_constraint(x, pltpu.HBM) for x in given]
    return pl.pallas_call(
        functools.partial(attend_kernel, axis_width),
        out_shape=halves
        + [pltpu.VMEM((2 * own_rows, extra_width), jnp.bfloat16)],
        in_specs=[pl.BlockSpec(memory_space=pltpu.HBM)] * len(given),
        out_specs=[pl.BlockSpec(memory_space=pltpu.VMEM)] * (2 * CHUNKS + 1),
        scratch_shapes=[space(x.shape, x.dtype) for space, x in zip(spaces, given)]
        + [pltpu.VMEM(queries.shape, jnp.bfloat16), pltpu.SemaphoreType.DMA((len(given),))],
        compiler_params=pltpu.CompilerParams(vmem_limit_bytes=16 * 1024 * 1024),
        name="attend",
    )(*given)


def feed_kernel(cut, tile, first, *refs):
    hidden, w_gate, w_up = refs[:3]
    before, after = ((), refs[3:]) if first else (refs[3:5], refs[5:])
    width = cut[1] - cut[0]
    for n in range(w_gate.shape[2] // tile):
        columns = slice(n * tile, (n + 1) * tile)
        for m, weights in enumerate((w_gate, w_up)):
            share = jnp.dot(
                hidden[:, :width],
                weights[0, cut[0] : cut[1], columns],
                preferred_element_type=jnp.float32,
            )
            after[m][:, columns] = share if first else before[m][:, columns] + share


def finish_kernel(axis_width, cut, out_cut, tile, hidden, w_gate, w_up, w_down, gate, up, *outs):
    kept, sent, activated, row_weight = outs
    f32, bf16 = jnp.float32, jnp.bfloat16
    width = cut[1] - cut[0]
    device = lax.axis_index("wide")
    parts = hidden[:, width:]
    lane = lax.broadcasted_iota(jnp.int32, parts.shape, 1)
    mine = (lane == device) | (lane == device + axis_width)
    weight = jnp.sum(jnp.where(mine, parts.astype(f32), 0.0), axis=1, keepdims=True)
    row_weight[...] = weight
    for n in range(w_gate.shape[2] // tile):
        columns = slice(n * tile, (n + 1) * tile)
        rows = hidden[:, :width]
        piece = slice(*cut)
        gate_part = gate[:, columns] + jnp.dot(
            rows, w_gate[0, piece, columns], preferred_element_type=f32
        )
        up_part = up[:, columns] + jnp.dot(
            rows, w_up[0, piece, columns], preferred_element_type=f32
        )
        activated[:, columns] = (gate_part / (1.0 + jnp.exp(-gate_part)) * up_part).astype(bf16)
    produce(activated, w_down.at[0, :, slice(*out_cut)], weight, kept, sent, tile)


def down_kernel(cut, tile, activated, row_weight, w_down, kept, sent):
    produce(activated, w_down.at[0, :, slice(*cut)], row_weight[...], kept, sent, tile)


def produce(activated, w_down, weight, kept, sent, tile):
    half, width = kept.shape
    for start in range(0, width, tile):
        columns = slice(start, min(start + tile, width))
        produced = jnp.dot(
            activated[...], w_down[:, columns], preferred_element_type=jnp.float32
        )
        weighted = produced * weight
        kept[:, columns] = weighted[:half]
        sent[:, columns] = weighted[half:].astype(jnp.bfloat16)


def local_call(kernel, name, out_shape, given):
    return pl.pallas_call(
        kernel,
        out_shape=out_shape,
        in_specs=[pl.BlockSpec(memory_space=pltpu.VMEM)] * len(given),
        out_specs=[pl.BlockSpec(memory_space=pltpu.VMEM)] * len(out_shape),
        compiler_params=pltpu.CompilerParams(vmem_limit_bytes=16 * 1024 * 1024),
        name=name,
    )(*given)


def experts(hidden, w_gate, w_up, w_down):
    axis_width = lax.axis_size("wide")
    rows = hidden[0].shape[0]
    hidden_width, features = w_down.shape[1:]
    cuts = column_cuts(features)
    tile = 256 if hidden_width % 256 == 0 else LANES
    wide = pltpu.VMEM((rows, hidden_width), jnp.float32)
    sums = []
    for c in range(CHUNKS - 1):
        given = [hidden[c], w_gate, w_up, *sums]
        kernel = functools.partial(feed_kernel, cuts[c], tile, c == 0)
        sums = local_call(kernel, "feed", [wide, wide], given)
    kept, sent, activated, row_weight = local_call(
        functools.partial(finish_kernel, axis_width, cuts[-1], cuts[0], tile),
        "finish",
        kept_and_sent(rows, cuts[:1])
        + [
            pltpu.VMEM((rows, hidden_width), jnp.bfloat16),
            pltpu.VMEM((rows, 1), jnp.float32),
        ],
        [hidden[-1], w_gate, w_up, w_down, *sums],
    )
    produced = [(kept, sent)]
    for c in range(1, CHUNKS):
        produced.append(
            local_call(
                functools.partial(down_kernel, cuts[c], tile),
                "down",
                kept_and_sent(rows, cuts[c : c + 1]),
                [activated, row_weight, w_down],
            )
        )
    return produced


def halved(block):
    half = block.shape[0] // 2
    return block[:half], block[half:].astype(jnp.bfloat16)


def body(
    queries,
    tree_kv,
    kv_cache,
    block_table,
    cache_lengths,
    parents,
    w_out,
    w_gate,
    w_up,
    w_down,
    expert_ids,
    gate_weights,
):
    axis_width = lax.axis_size("wide")
    steps = list(zip(*slice_orders(axis_width)))
    group_steps = [(1 << k, 1 << k) for k in range(bits_of(axis_width // ATT_TP))]
    *halves, extra = attend(
        queries, tree_kv, kv_cache, block_table, cache_lengths, parents, w_out,
        expert_ids, gate_weights,
    )
    hidden = []
    for c in range(CHUNKS):
        kept, sent = halves[2 * c], halves[2 * c + 1]
        for number, masks in enumerate(steps[:-1]):
            kept = kept + exchange(sent, masks).astype(jnp.float32)
            if number < len(steps) - 2:
                kept, sent = halved(kept)
        if c == CHUNKS - 1:
            kept = jnp.concatenate([kept, extra.astype(jnp.float32)], axis=1)
        half = kept.shape[0] // 2
        other = exchange(kept.astype(jnp.bfloat16), steps[-1]).astype(jnp.float32)
        block = kept + jnp.concatenate([other[half:], other[:half]], axis=0)
        block = block.astype(jnp.bfloat16)
        for masks in steps[-2::-1] + group_steps:
            block = jnp.concatenate([block, exchange(block, masks)], axis=0)
        hidden.append(block)
    produced = experts(hidden, w_gate, w_up, w_down)
    results = []
    for c in range(CHUNKS):
        kept, sent = produced[c]
        last = len(group_steps) + len(steps) - 1
        for number, masks in enumerate(group_steps[::-1] + steps):
            kept = kept + exchange(sent, masks).astype(jnp.float32)
            if number < last:
                kept, sent = halved(kept)
        results.append(kept.astype(jnp.bfloat16))
    return jnp.concatenate(results, axis=1)


def solution(mesh):
    placed = (
        P(("groups", "wide"), None),
        P(None, ("groups", "wide"), None),
        P(None, ("groups", "wide"), None, None),
        P(("groups", "wide"), None),
        P(("groups", "wide"), None),
        P(("groups", "wide"), None),
        P("wide", None),
        P("wide", None, None),
        P("wide", None, None),
        P("wide", None, None),
        P(("groups", "wide"), None),
        P(("groups", "wide"), None),
    )
    return jax.shard_map(
        body, mesh=mesh, in_specs=placed, out_specs=P(("groups", "wide"), None), check_vma=False
    )
```

```python
import functools

import jax
import jax.numpy as jnp
from jax import lax
from jax.experimental import pallas as pl
from jax.experimental.pallas import tpu as pltpu
from jax.sharding import PartitionSpec as P

ATT_TP = 8
PIECES = (8, 8)
CHUNKS = len(PIECES)
CARRIER = 0
LANES = 128


def bits_of(count):
    return count.bit_length() - 1


def column_cuts(features):
    ends = [features * sum(PIECES[: c + 1]) // sum(PIECES) for c in range(CHUNKS)]
    return list(zip([0] + ends[:-1], ends))


def spare_width(axis_width):
    return -(-2 * axis_width // LANES) * LANES


def exchange(block, masks):
    count = lax.axis_size("wide")
    return lax.ppermute(block, "wide", [(i, i ^ masks[i & 1]) for i in range(count)])


def slice_orders(axis_width):
    groups = axis_width // ATT_TP
    first = [groups << step for step in range(bits_of(ATT_TP))]
    second = [first[1], first[0]] + first[2:] if groups > 1 and len(first) > 2 else first
    return first, second


def relative_masks(order):
    steps = len(order)
    masks = []
    for j in range(1 << steps):
        mask = 0
        for step in range(steps):
            if j >> (steps - 1 - step) & 1:
                mask ^= order[step]
        masks.append(mask)
    return masks


def attend_kernel(axis_width, *refs):
    sources, outs, scratch = refs[:10], refs[10 : 12 + 2 * CHUNKS], refs[12 + 2 * CHUNKS :]
    *inputs, attended, sems = scratch
    copies = [
        pltpu.make_async_copy(source, target, sems.at[n])
        for n, (source, target) in enumerate(zip(sources, [*inputs, outs[-1]]))
    ]
    for copy in copies:
        copy.start()
    for copy in copies[:-2]:
        copy.wait()
    table, lengths, parents, expert_ids, gate_weights = inputs[:5]
    queries, tree_kv, kv_cache, weights_in = inputs[5:]
    *outs, extra, w_down = outs
    seq_count, node_count = parents.shape
    head_dim = tree_kv.shape[-1]
    head_count = queries.shape[1] // head_dim
    pages = table.shape[1]
    cached = pages * kv_cache.shape[2]
    all_nodes = seq_count * node_count
    query_count = head_count * node_count
    f32, bf16 = jnp.float32, jnp.bfloat16

    shifted = [
        jnp.where(parents[s : s + 1, :] >= 0, parents[s : s + 1, :] + s * node_count, -1)
        for s in range(seq_count)
    ]
    parent_row = jnp.concatenate(shifted, axis=1)
    rows = lax.broadcasted_iota(jnp.int32, (all_nodes, all_nodes), 0)
    columns = lax.broadcasted_iota(jnp.int32, (all_nodes, all_nodes), 1)
    reached = ((rows == columns) | (rows == parent_row)).astype(f32).astype(bf16)
    for repeat in range(max(node_count - 1, 1).bit_length()):
        squared = jnp.dot(reached, reached, preferred_element_type=f32)
        reached = jnp.minimum(squared, 1.0).astype(bf16)

    node_rows = lax.broadcasted_iota(jnp.int32, (all_nodes, query_count), 0)
    query_nodes = lax.broadcasted_iota(jnp.int32, (all_nodes, query_count), 1) % node_count
    positions = lax.broadcasted_iota(jnp.int32, (cached, query_count), 0)
    for s in range(seq_count):
        own = slice(s * node_count, (s + 1) * node_count)
        spread = (node_rows == query_nodes + s * node_count).astype(f32).astype(bf16)
        tree_open = jnp.dot(reached[own], spread, preferred_element_type=f32) > 0.5
        keys = [kv_cache[0, table[s, p]] for p in range(pages)]
        values = [kv_cache[1, table[s, p]] for p in range(pages)]
        key_rows = jnp.concatenate(keys + [tree_kv[0, own]], axis=0)
        value_rows = jnp.concatenate(values + [tree_kv[1, own]], axis=0)
        query_rows = jnp.concatenate(
            [queries[own, h * head_dim : (h + 1) * head_dim] for h in range(head_count)], axis=0
        )
        scores = lax.dot_general(
            key_rows, query_rows, (((1,), (1,)), ((), ())), preferred_element_type=f32
        ) * head_dim ** (-0.5)
        cache_scores = jnp.where(positions < lengths[0, s], scores[:cached], -jnp.inf)
        tree_scores = jnp.where(tree_open, scores[cached:], -jnp.inf)
        masked = jnp.concatenate([cache_scores, tree_scores], axis=0)
        highest = jnp.max(masked, axis=0, keepdims=True)
        probs = jnp.exp(masked - highest)
        total = jnp.broadcast_to(jnp.sum(probs, axis=0, keepdims=True), (head_dim, query_count))
        blended = lax.dot_general(
            probs.astype(bf16), value_rows, (((0,), (0,)), ((), ())), preferred_element_type=f32
        )
        blended = (blended / total.T).astype(bf16)
        for h in range(head_count):
            attended[own, h * head_dim : (h + 1) * head_dim] = blended[
                h * node_count : (h + 1) * node_count
            ]

    listed, row_count = expert_ids.shape
    spread_width = extra.shape[1]
    expert = lax.broadcasted_iota(jnp.int32, (spread_width, row_count), 0)
    weight = jnp.zeros((spread_width, row_count), f32)
    for k in range(listed):
        weight += jnp.where(
            expert_ids[k : k + 1, :] == expert % axis_width, gate_weights[k : k + 1, :], 0.0
        )
    upper = weight.astype(bf16).astype(f32)
    parts = jnp.where(
        expert < axis_width, upper, jnp.where(expert < 2 * axis_width, weight - upper, 0.0)
    )
    extra[:row_count] = parts.T.astype(bf16)
    extra[row_count:] = jnp.zeros((row_count, spread_width), bf16)

    device = lax.axis_index("wide")
    groups = axis_width // ATT_TP
    first, second = [relative_masks(order) for order in slice_orders(axis_width)]
    block = all_nodes // ATT_TP
    picked = []
    for one, other in zip(first, second):
        target = (device ^ jnp.where(device & 1 == 0, one, other)) // groups
        picked.append(attended[pl.ds(pl.multiple_of(target * block, block), block), :])
    ordered = jnp.concatenate(picked, axis=0)
    copies[-2].wait()
    half = all_nodes // 2
    for c, (low, high) in enumerate(column_cuts(weights_in.shape[1])):
        projected = jnp.dot(ordered, weights_in[:, low:high], preferred_element_type=f32)
        outs[2 * c][...] = projected[:half]
        outs[2 * c + 1][...] = projected[half:].astype(bf16)
    copies[-1].wait()


def kept_and_sent(rows, cuts):
    shapes = []
    for low, high in cuts:
        shapes.append(pltpu.VMEM((rows // 2, high - low), jnp.float32))
        shapes.append(pltpu.VMEM((rows // 2, high - low), jnp.bfloat16))
    return shapes


def attend(
    queries, tree_kv, kv_cache, table, lengths, parents, w_out, w_down, expert_ids, gate_weights
):
    axis_width = lax.axis_size("wide")
    features = w_out.shape[1]
    rows = queries.shape[0]
    own_rows = expert_ids.shape[0]
    extra_width = spare_width(axis_width)
    halves = kept_and_sent(rows, column_cuts(features))
    given = [table, lengths, parents, expert_ids.T, gate_weights.T, queries, tree_kv, kv_cache, w_out, w_down]
    spaces = [pltpu.SMEM] * 2 + [pltpu.VMEM] * (len(given) - 2)
    given = [pltpu.with_memory_space_constraint(x, pltpu.HBM) for x in given]
    return pl.pallas_call(
        functools.partial(attend_kernel, axis_width),
        out_shape=halves
        + [pltpu.VMEM((2 * own_rows, extra_width), jnp.bfloat16), pltpu.VMEM(w_down.shape, w_down.dtype)],
        in_specs=[pl.BlockSpec(memory_space=pltpu.HBM)] * len(given),
        out_specs=[pl.BlockSpec(memory_space=pltpu.VMEM)] * (2 * CHUNKS + 2),
        scratch_shapes=[space(x.shape, x.dtype) for space, x in zip(spaces, given[:-1])]
        + [pltpu.VMEM(queries.shape, jnp.bfloat16), pltpu.SemaphoreType.DMA((len(given),))],
        compiler_params=pltpu.CompilerParams(vmem_limit_bytes=16 * 1024 * 1024),
        name="attend",
    )(*given)


def feed_kernel(cut, tile, pairs, first, *refs):
    hidden, weights, refs = refs[:2], refs[2 : 2 + pairs], refs[2 + pairs :]
    before, after = (None, refs) if first else (refs[:pairs], refs[pairs:])
    rows = jnp.concatenate([half[:, : cut[1] - cut[0]] for half in hidden], axis=0)
    for m in range(pairs):
        for n in range(weights[m].shape[2] // tile):
            columns = slice(n * tile, (n + 1) * tile)
            share = jnp.dot(
                rows, weights[m][0, cut[0] : cut[1], columns], preferred_element_type=jnp.float32
            )
            after[m][:, columns] = share if first else before[m][:, columns] + share


def finish_kernel(axis_width, spare, cut, out_cut, tile, owners, *refs):
    count = len(owners)
    hidden, carrier, refs = refs[:2], refs[2:4], refs[4:]
    feeds, downs, sums = refs[: 2 * count], refs[2 * count : 3 * count], refs[3 * count : 5 * count]
    kept, sent = refs[5 * count : 5 * count + 2]
    activated, row_weight = refs[5 * count + 2 : 6 * count + 2], refs[6 * count + 2 :]
    f32, bf16 = jnp.float32, jnp.bfloat16
    width = cut[1] - cut[0]
    device = lax.axis_index("wide")
    rows = jnp.concatenate([half[:, :width] for half in hidden], axis=0)
    parts = jnp.concatenate([half[:, -spare:] for half in carrier], axis=0)
    lane = lax.broadcasted_iota(jnp.int32, parts.shape, 1)
    piece = slice(*cut)
    for m, owner in enumerate(owners):
        expert = device ^ owner
        mine = (lane == expert) | (lane == expert + axis_width)
        row_weight[m][...] = jnp.sum(jnp.where(mine, parts.astype(f32), 0.0), axis=1, keepdims=True)
        for n in range(feeds[2 * m].shape[2] // tile):
            columns = slice(n * tile, (n + 1) * tile)
            gate_part, up_part = [
                sums[2 * m + k][:, columns]
                + jnp.dot(rows, feeds[2 * m + k][0, piece, columns], preferred_element_type=f32)
                for k in range(2)
            ]
            activated[m][:, columns] = (
                gate_part / (1.0 + jnp.exp(-gate_part)) * up_part
            ).astype(bf16)
    produce(activated, downs, row_weight, out_cut, kept, sent, tile)


def down_kernel(cut, tile, count, *refs):
    activated, row_weight, downs = [refs[k * count : (k + 1) * count] for k in range(3)]
    produce(activated, downs, row_weight, cut, *refs[3 * count :], tile)


def produce(activated, downs, row_weight, cut, kept, sent, tile):
    half, width = kept.shape
    for start in range(0, width, tile):
        size = min(tile, width - start)
        columns = slice(cut[0] + start, cut[0] + start + size)
        weighted = 0.0
        for rows, w_down, weight in zip(activated, downs, row_weight):
            weighted += (
                jnp.dot(rows[...], w_down[0, :, columns], preferred_element_type=jnp.float32)
                * weight[...]
            )
        kept[:, start : start + size] = weighted[:half]
        sent[:, start : start + size] = weighted[half:].astype(jnp.bfloat16)


def local_call(kernel, name, out_shape, given):
    return pl.pallas_call(
        kernel,
        out_shape=out_shape,
        in_specs=[pl.BlockSpec(memory_space=pltpu.VMEM)] * len(given),
        out_specs=[pl.BlockSpec(memory_space=pltpu.VMEM)] * len(out_shape),
        compiler_params=pltpu.CompilerParams(vmem_limit_bytes=16 * 1024 * 1024),
        name=name,
    )(*given)


def experts(hidden, owners, feeds, downs):
    axis_width = lax.axis_size("wide")
    rows = 2 * hidden[0][0].shape[0]
    hidden_width, features = downs[0].shape[1:]
    cuts = column_cuts(features)
    spare = spare_width(axis_width)
    count = len(owners)
    tile = 256 if hidden_width % 256 == 0 else LANES
    wide = pltpu.VMEM((rows, hidden_width), jnp.float32)
    sums = []
    for c in range(CHUNKS - 1):
        kernel = functools.partial(feed_kernel, cuts[c], tile, 2 * count, c == 0)
        sums = local_call(kernel, "feed", [wide] * (2 * count), [*hidden[c], *feeds, *sums])
    kept, sent, *rest = local_call(
        functools.partial(finish_kernel, axis_width, spare, cuts[-1], cuts[0], tile, owners),
        "finish",
        kept_and_sent(rows, cuts[:1])
        + [pltpu.VMEM((rows, hidden_width), jnp.bfloat16)] * count
        + [pltpu.VMEM((rows, 1), jnp.float32)] * count,
        [*hidden[-1], *hidden[CARRIER], *feeds, *downs, *sums],
    )
    produced = [(kept, sent)]
    for c in range(1, CHUNKS):
        kernel = functools.partial(down_kernel, cuts[c], tile, count)
        shapes = kept_and_sent(rows, cuts[c : c + 1])
        produced.append(local_call(kernel, "down", shapes, [*rest, *downs]))
    return produced


def halved(block):
    half = block.shape[0] // 2
    return block[:half], block[half:].astype(jnp.bfloat16)


def ordered_after(value, earlier):
    return value if earlier is None else lax.optimization_barrier((value, earlier))[0]


def reduce_and_gather(halves, extra, steps, gathers):
    f32, bf16 = jnp.float32, jnp.bfloat16
    parts = [list(halves[2 * c : 2 * c + 2]) for c in range(CHUNKS)]
    for number, masks in enumerate(steps[:-1]):
        earlier = None
        for c, part in enumerate(parts):
            kept, sent = part
            kept = kept + ordered_after(exchange(sent, masks), earlier).astype(f32)
            if number < len(steps) - 2:
                part[:] = halved(kept)
            else:
                if c == CARRIER:
                    kept = jnp.concatenate([kept, extra.astype(f32)], axis=1)
                part[:] = kept, kept.astype(bf16)
            earlier = part[1]
    blocks, earlier = [], None
    for kept, sent in parts:
        half = kept.shape[0] // 2
        other = ordered_after(exchange(sent, steps[-1]), earlier).astype(f32)
        blocks.append((kept + jnp.concatenate([other[half:], other[:half]], axis=0)).astype(bf16))
        earlier = blocks[-1]
    for masks in gathers[:-1]:
        earlier = None
        for c, block in enumerate(blocks):
            other = ordered_after(exchange(block, masks), earlier)
            blocks[c] = earlier = jnp.concatenate([block, other], axis=0)
    return [(block, exchange(block, gathers[-1])) for block in blocks]


def body(
    queries,
    tree_kv,
    kv_cache,
    block_table,
    cache_lengths,
    parents,
    w_out,
    w_gate,
    w_up,
    w_down,
    expert_ids,
    gate_weights,
):
    axis_width = lax.axis_size("wide")
    steps = list(zip(*slice_orders(axis_width)))
    group_steps = [(1 << k, 1 << k) for k in range(1, bits_of(axis_width // ATT_TP))]
    pair = (1, 1)
    owners = (0, 1)
    feeds = [w_gate, w_up, exchange(w_gate, pair), exchange(w_up, pair)]
    *halves, extra, fetched = attend(
        queries, tree_kv, kv_cache, block_table, cache_lengths, parents, w_out, w_down,
        expert_ids, gate_weights,
    )
    downs = [fetched, exchange(w_down, pair)]
    gathers = steps[-2::-1] + group_steps
    hidden = reduce_and_gather(halves, extra, steps, gathers)
    produced = experts(hidden, owners, feeds, downs)
    results = []
    parts = [list(pair) for pair in produced]
    hops = group_steps[::-1] + steps
    for number, masks in enumerate(hops):
        earlier = None
        for part in parts:
            kept, sent = part
            other = ordered_after(exchange(sent, masks), earlier)
            kept = kept + other.astype(jnp.float32)
            if number < len(hops) - 1:
                part[:] = halved(kept)
                earlier = part[1]
            else:
                results.append(kept.astype(jnp.bfloat16))
                earlier = results[-1]
    return jnp.concatenate(results, axis=1)


def solution(mesh):
    placed = (
        P(("groups", "wide"), None),
        P(None, ("groups", "wide"), None),
        P(None, ("groups", "wide"), None, None),
        P(("groups", "wide"), None),
        P(("groups", "wide"), None),
        P(("groups", "wide"), None),
        P("wide", None),
        P("wide", None, None),
        P("wide", None, None),
        P("wide", None, None),
        P(("groups", "wide"), None),
        P(("groups", "wide"), None),
    )
    return jax.shard_map(
        body, mesh=mesh, in_specs=placed, out_specs=P(("groups", "wide"), None), check_vma=False
    )
```

```python
import functools

import jax
import jax.numpy as jnp
from jax import lax
from jax.experimental import pallas as pl
from jax.experimental.pallas import tpu as pltpu
from jax.sharding import PartitionSpec as P

ATT_TP = 8
PIECES = (8, 8)
CHUNKS = len(PIECES)
CARRIER = 0
LANES = 128
HINT = 30_000_000_000


def bits_of(count):
    return count.bit_length() - 1


def column_cuts(features):
    ends = [features * sum(PIECES[: c + 1]) // sum(PIECES) for c in range(CHUNKS)]
    return list(zip([0] + ends[:-1], ends))


def spare_width(axis_width):
    return -(-2 * axis_width // LANES) * LANES


def slice_orders(axis_width):
    groups = axis_width // ATT_TP
    first = [groups << step for step in range(bits_of(ATT_TP))]
    second = [first[1], first[0], *first[2:]]
    return first, second


def exchange(block, route):
    count = lax.axis_size("wide")
    return lax.ppermute(block, "wide", [(i, route(i)) for i in range(count)])


def on_odd_chip():
    index = lax.axis_index("wide") // (lax.axis_size("wide") // ATT_TP)
    odd = 0
    for step in range(bits_of(ATT_TP)):
        odd ^= index >> step & 1
    return odd == 1


class Routes:
    def __init__(self, axis_width):
        groups = axis_width // ATT_TP
        orders = slice_orders(axis_width)
        odd = lambda i: (i // groups).bit_count() & 1
        self.pair = lambda i: i ^ 1
        self.steps = [
            lambda i, step=step: i ^ orders[(i & 1) ^ odd(i)][step] ^ 1
            for step in range(bits_of(ATT_TP))
        ]
        self.last = lambda i: i ^ orders[(i & 1) ^ odd(i)][-1] ^ odd(i)
        self.groups = [lambda i, k=k: i ^ 1 << k for k in range(1, bits_of(groups))]


def relative_masks(order):
    steps = len(order)
    masks = []
    for j in range(1 << steps):
        mask = 0
        for step in range(steps):
            if j >> (steps - 1 - step) & 1:
                mask ^= order[step]
        masks.append(mask)
    return masks


def started(sources, targets, sems):
    copies = [
        pltpu.make_async_copy(source, target, sems.at[n])
        for n, (source, target) in enumerate(zip(sources, targets))
    ]
    for copy in copies:
        copy.start()
    return copies


def attend_kernel(axis_width, *refs):
    sources, (ordered, w_out, w_down), scratch = refs[:10], refs[10:13], refs[13:]
    *inputs, attended, sems = scratch
    copies = started(sources, [*inputs, w_out, w_down], sems)
    for copy in copies[:-2]:
        copy.wait()
    table, lengths, parents, expert_ids, gate_weights, queries, tree_kv, kv_cache = inputs
    seq_count, node_count = parents.shape
    head_dim = tree_kv.shape[-1]
    head_count = queries.shape[1] // head_dim
    pages = table.shape[1]
    cached = pages * kv_cache.shape[2]
    all_nodes = seq_count * node_count
    query_count = head_count * node_count
    f32, bf16 = jnp.float32, jnp.bfloat16

    lane = lax.broadcasted_iota(jnp.int32, (8, all_nodes), 1)
    shifted = [
        jnp.where(parents[s : s + 1, :] >= 0, parents[s : s + 1, :] + s * node_count, -1)
        for s in range(seq_count)
    ]
    above = jnp.broadcast_to(jnp.concatenate(shifted, axis=1), lane.shape)
    above = jnp.where(above >= 0, above, lane)
    words = jnp.left_shift(1, lane % node_count)
    for repeat in range(max(node_count - 1, 1).bit_length()):
        words = words | jnp.take_along_axis(words, above, axis=1)
        above = jnp.take_along_axis(above, above, axis=1)

    query_nodes = lax.broadcasted_iota(jnp.int32, (8, query_count), 1) % node_count
    node_rows = lax.broadcasted_iota(jnp.int32, (node_count, query_count), 0)
    positions = lax.broadcasted_iota(jnp.int32, (cached, query_count), 0)
    for s in range(seq_count):
        own = slice(s * node_count, (s + 1) * node_count)
        word = jnp.take_along_axis(words, query_nodes + s * node_count, axis=1)
        word = jnp.broadcast_to(word[:1], node_rows.shape)
        tree_open = (lax.shift_right_logical(word, node_rows) & 1) == 1
        keys = [kv_cache[0, table[s, p]] for p in range(pages)]
        values = [kv_cache[1, table[s, p]] for p in range(pages)]
        key_rows = jnp.concatenate(keys + [tree_kv[0, own]], axis=0)
        value_rows = jnp.concatenate(values + [tree_kv[1, own]], axis=0)
        query_rows = jnp.concatenate(
            [queries[own, h * head_dim : (h + 1) * head_dim] for h in range(head_count)], axis=0
        )
        scores = lax.dot_general(
            key_rows, query_rows, (((1,), (1,)), ((), ())), preferred_element_type=f32
        ) * head_dim ** (-0.5)
        cache_scores = jnp.where(positions < lengths[0, s], scores[:cached], -jnp.inf)
        tree_scores = jnp.where(tree_open, scores[cached:], -jnp.inf)
        masked = jnp.concatenate([cache_scores, tree_scores], axis=0)
        highest = jnp.max(masked, axis=0, keepdims=True)
        probs = jnp.exp(masked - highest)
        total = jnp.broadcast_to(jnp.sum(probs, axis=0, keepdims=True), (head_dim, query_count))
        blended = lax.dot_general(
            probs.astype(bf16), value_rows, (((0,), (0,)), ((), ())), preferred_element_type=f32
        )
        blended = (blended / total.T).astype(bf16)
        for h in range(head_count):
            attended[own, h * head_dim : (h + 1) * head_dim] = blended[
                h * node_count : (h + 1) * node_count
            ]

    listed, row_count = expert_ids.shape
    spread_width = spare_width(axis_width)
    expert = lax.broadcasted_iota(jnp.int32, (spread_width, row_count), 0)
    weight = jnp.zeros((spread_width, row_count), f32)
    for k in range(listed):
        weight += jnp.where(
            expert_ids[k : k + 1, :] == expert % axis_width, gate_weights[k : k + 1, :], 0.0
        )
    upper = weight.astype(bf16).astype(f32)
    parts = jnp.where(
        expert < axis_width, upper, jnp.where(expert < 2 * axis_width, weight - upper, 0.0)
    )
    ordered[:row_count, -spread_width:] = parts.T.astype(bf16)
    rest = (all_nodes - row_count, spread_width)
    ordered[row_count:, -spread_width:] = jnp.zeros(rest, bf16)

    device = lax.axis_index("wide")
    groups = axis_width // ATT_TP
    first, second = [relative_masks(order) for order in slice_orders(axis_width)]
    block = all_nodes // ATT_TP
    picked = []
    for one, other in zip(first, second):
        target = (device ^ jnp.where(device & 1 == 0, one, other)) // groups
        picked.append(attended[pl.ds(pl.multiple_of(target * block, block), block), :])
    ordered[:, : queries.shape[1]] = jnp.concatenate(picked, axis=0)
    for copy in copies[-2:]:
        copy.wait()


def project_kernel(own_rows, cut, own, other, w_out, kept, sent, *extra):
    rows = jnp.where(on_odd_chip(), other[...], own[...])
    width = w_out.shape[0]
    if extra:
        extra[0][...] = rows[: 2 * own_rows, width:]
    half = rows.shape[0] // 2
    projected = jnp.dot(
        rows[:, :width], w_out[:, cut[0] : cut[1]], preferred_element_type=jnp.float32
    )
    kept[...] = projected[:half]
    sent[...] = projected[half:].astype(jnp.bfloat16)


def project(own, other, w_out, own_rows):
    spare = spare_width(lax.axis_size("wide"))
    halves = []
    for c, cut in enumerate(column_cuts(w_out.shape[1])):
        shapes = kept_and_sent(own.shape[0], [cut])
        last = c == CHUNKS - 1
        halves += local_call(
            functools.partial(project_kernel, own_rows, cut),
            "project",
            shapes + [pltpu.VMEM((2 * own_rows, spare), jnp.bfloat16)] * last,
            [own, other, w_out],
            flops=HINT * c,
        )
    return halves


def kept_and_sent(rows, cuts):
    shapes = []
    for low, high in cuts:
        shapes.append(pltpu.VMEM((rows // 2, high - low), jnp.float32))
        shapes.append(pltpu.VMEM((rows // 2, high - low), jnp.bfloat16))
    return shapes


def attend(
    queries, tree_kv, kv_cache, table, lengths, parents, w_out, w_down, expert_ids, gate_weights
):
    axis_width = lax.axis_size("wide")
    rows, width = queries.shape
    given = [table, lengths, parents, expert_ids.T, gate_weights.T, queries, tree_kv, kv_cache, w_out, w_down]
    spaces = [pltpu.SMEM] * 2 + [pltpu.VMEM] * 6
    given = [pltpu.with_memory_space_constraint(x, pltpu.HBM) for x in given]
    return pl.pallas_call(
        functools.partial(attend_kernel, axis_width),
        out_shape=[
            pltpu.VMEM((rows, width + spare_width(axis_width)), jnp.bfloat16),
            pltpu.VMEM(w_out.shape, w_out.dtype),
            pltpu.VMEM(w_down.shape, w_down.dtype),
        ],
        in_specs=[pl.BlockSpec(memory_space=pltpu.HBM)] * len(given),
        out_specs=[pl.BlockSpec(memory_space=pltpu.VMEM)] * 3,
        scratch_shapes=[space(x.shape, x.dtype) for space, x in zip(spaces, given)]
        + [pltpu.VMEM(queries.shape, jnp.bfloat16), pltpu.SemaphoreType.DMA((len(given),))],
        compiler_params=pltpu.CompilerParams(vmem_limit_bytes=16 * 1024 * 1024),
        name="attend",
    )(*given)


def feed_kernel(cut, tile, pairs, first, *refs):
    hidden, weights, refs = refs[:2], refs[2 : 2 + pairs], refs[2 + pairs :]
    before, after = (None, refs) if first else (refs[:pairs], refs[pairs:])
    rows = jnp.concatenate([half[:, : cut[1] - cut[0]] for half in hidden], axis=0)
    for m in range(pairs):
        for n in range(weights[m].shape[2] // tile):
            columns = slice(n * tile, (n + 1) * tile)
            share = jnp.dot(
                rows, weights[m][0, cut[0] : cut[1], columns], preferred_element_type=jnp.float32
            )
            after[m][:, columns] = share if first else before[m][:, columns] + share


def finish_kernel(axis_width, spare, cut, out_cut, tile, owners, *refs):
    count = len(owners)
    hidden, carrier, refs = refs[:2], refs[2:4], refs[4:]
    feeds, downs, sums = refs[: 2 * count], refs[2 * count : 3 * count], refs[3 * count : 5 * count]
    kept, sent = refs[5 * count : 5 * count + 2]
    activated, row_weight = refs[5 * count + 2 : 6 * count + 2], refs[6 * count + 2 :]
    f32, bf16 = jnp.float32, jnp.bfloat16
    width = cut[1] - cut[0]
    device = lax.axis_index("wide")
    rows = jnp.concatenate([half[:, :width] for half in hidden], axis=0)
    parts = jnp.concatenate([half[:, -spare:] for half in carrier], axis=0)
    lane = lax.broadcasted_iota(jnp.int32, parts.shape, 1)
    piece = slice(*cut)
    for m, owner in enumerate(owners):
        expert = device ^ owner
        mine = (lane == expert) | (lane == expert + axis_width)
        row_weight[m][...] = jnp.sum(jnp.where(mine, parts.astype(f32), 0.0), axis=1, keepdims=True)
        for n in range(feeds[2 * m].shape[2] // tile):
            columns = slice(n * tile, (n + 1) * tile)
            gate_part, up_part = [
                sums[2 * m + k][:, columns]
                + jnp.dot(rows, feeds[2 * m + k][0, piece, columns], preferred_element_type=f32)
                for k in range(2)
            ]
            activated[m][:, columns] = (
                gate_part / (1.0 + jnp.exp(-gate_part)) * up_part
            ).astype(bf16)
    produce(activated, downs, row_weight, out_cut, kept, sent, tile)


def down_kernel(cut, tile, count, *refs):
    activated, row_weight, downs = [refs[k * count : (k + 1) * count] for k in range(3)]
    produce(activated, downs, row_weight, cut, *refs[3 * count :], tile)


def produce(activated, downs, row_weight, cut, kept, sent, tile):
    half, width = kept.shape
    for start in range(0, width, tile):
        size = min(tile, width - start)
        columns = slice(cut[0] + start, cut[0] + start + size)
        weighted = 0.0
        for rows, w_down, weight in zip(activated, downs, row_weight):
            weighted += (
                jnp.dot(rows[...], w_down[0, :, columns], preferred_element_type=jnp.float32)
                * weight[...]
            )
        kept[:, start : start + size] = weighted[:half]
        sent[:, start : start + size] = weighted[half:].astype(jnp.bfloat16)


def local_call(kernel, name, out_shape, given, flops=0):
    return pl.pallas_call(
        kernel,
        out_shape=out_shape,
        in_specs=[pl.BlockSpec(memory_space=pltpu.VMEM)] * len(given),
        out_specs=[pl.BlockSpec(memory_space=pltpu.VMEM)] * len(out_shape),
        compiler_params=pltpu.CompilerParams(vmem_limit_bytes=16 * 1024 * 1024),
        cost_estimate=pl.CostEstimate(flops=flops, bytes_accessed=0, transcendentals=0) if flops else None,
        name=name,
    )(*given)


def experts(hidden, owners, feeds, downs):
    axis_width = lax.axis_size("wide")
    rows = 2 * hidden[0][0].shape[0]
    hidden_width, features = downs[0].shape[1:]
    cuts = column_cuts(features)
    spare = spare_width(axis_width)
    count = len(owners)
    tile = 256 if hidden_width % 256 == 0 else LANES
    wide = pltpu.VMEM((rows, hidden_width), jnp.float32)
    sums = []
    for c in range(CHUNKS - 1):
        kernel = functools.partial(feed_kernel, cuts[c], tile, 2 * count, c == 0)
        sums = local_call(kernel, "feed", [wide] * (2 * count), [*hidden[c], *feeds, *sums])
    kept, sent, *rest = local_call(
        functools.partial(finish_kernel, axis_width, spare, cuts[-1], cuts[0], tile, owners),
        "finish",
        kept_and_sent(rows, cuts[:1])
        + [pltpu.VMEM((rows, hidden_width), jnp.bfloat16)] * count
        + [pltpu.VMEM((rows, 1), jnp.float32)] * count,
        [*hidden[-1], *hidden[CARRIER], *feeds, *downs, *sums],
    )
    produced = [(kept, sent)]
    for c in range(1, CHUNKS):
        kernel = functools.partial(down_kernel, cuts[c], tile, count)
        shapes = kept_and_sent(rows, cuts[c : c + 1])
        produced.append(local_call(kernel, "down", shapes, [*rest, *downs]))
    return produced


def halved(block):
    half = block.shape[0] // 2
    return block[:half], block[half:].astype(jnp.bfloat16)


def ordered_after(value, earlier):
    return value if earlier is None else lax.optimization_barrier((value, earlier))[0]


def reduce_and_gather(halves, extra, routes):
    f32, bf16 = jnp.float32, jnp.bfloat16
    parts = [list(halves[2 * c : 2 * c + 2]) for c in range(CHUNKS)]
    for number, route in enumerate(routes.steps[:-1]):
        earlier = None
        for c, part in enumerate(parts):
            kept, sent = part
            kept = kept + ordered_after(exchange(sent, route), earlier).astype(f32)
            if number < len(routes.steps) - 2:
                part[:] = halved(kept)
            else:
                if c == CARRIER:
                    kept = jnp.concatenate([kept, extra.astype(f32)], axis=1)
                part[:] = kept, kept.astype(bf16)
            earlier = part[1]
    blocks, earlier = [], None
    for kept, sent in parts:
        half = kept.shape[0] // 2
        other = ordered_after(exchange(sent, routes.steps[-1]), earlier).astype(f32)
        blocks.append((kept + jnp.concatenate([other[half:], other[:half]], axis=0)).astype(bf16))
        earlier = blocks[-1]
    gathers = routes.steps[-2::-1] + routes.groups
    for route in gathers[:-1]:
        earlier = None
        for c, block in enumerate(blocks):
            other = ordered_after(exchange(block, route), earlier)
            blocks[c] = earlier = jnp.concatenate([block, other], axis=0)
    return [(block, exchange(block, gathers[-1])) for block in blocks]


def body(
    queries,
    tree_kv,
    kv_cache,
    block_table,
    cache_lengths,
    parents,
    w_out,
    w_gate,
    w_up,
    w_down,
    expert_ids,
    gate_weights,
):
    axis_width = lax.axis_size("wide")
    routes = Routes(axis_width)
    owners = (0, 1)
    own, fetched_out, fetched_down = attend(
        queries, tree_kv, kv_cache, block_table, cache_lengths, parents, w_out, w_down,
        expert_ids, gate_weights,
    )
    *halves, extra = project(own, exchange(own, routes.pair), fetched_out, expert_ids.shape[0])
    others = [exchange(x, routes.pair) for x in (w_gate, w_up, w_down)]
    feeds = [w_gate, w_up, *others[:2]]
    downs = [fetched_down, others[2]]
    hidden = reduce_and_gather(halves, extra, routes)
    parts = [list(pair) for pair in experts(hidden, owners, feeds, downs)]
    for route in routes.groups[::-1] + routes.steps[:-1]:
        earlier = None
        for part in parts:
            kept, sent = part
            other = ordered_after(exchange(sent, route), earlier)
            part[:] = halved(kept + other.astype(jnp.float32))
            earlier = part[1]
    results, earlier = [], None
    for kept, sent in parts:
        other = ordered_after(exchange(sent, routes.steps[-1]), earlier).astype(jnp.float32)
        results.append((kept + other).astype(jnp.bfloat16))
        earlier = results[-1]
    result = jnp.concatenate(results, axis=1)
    return jnp.where(on_odd_chip(), exchange(result, routes.pair), result)


def solution(mesh):
    placed = (
        P(("groups", "wide"), None),
        P(None, ("groups", "wide"), None),
        P(None, ("groups", "wide"), None, None),
        P(("groups", "wide"), None),
        P(("groups", "wide"), None),
        P(("groups", "wide"), None),
        P("wide", None),
        P("wide", None, None),
        P("wide", None, None),
        P("wide", None, None),
        P(("groups", "wide"), None),
        P(("groups", "wide"), None),
    )
    return jax.shard_map(
        body, mesh=mesh, in_specs=placed, out_specs=P(("groups", "wide"), None), check_vma=False
    )
```

```python
import functools

import jax
import jax.numpy as jnp
from jax import lax
from jax.experimental import pallas as pl
from jax.experimental.pallas import tpu as pltpu
from jax.sharding import PartitionSpec as P

ATT_TP = 8
PIECES = (8, 8)
CHUNKS = len(PIECES)
CARRIER = 0
LANES = 128
HINT = 30_000_000_000


def bits_of(count):
    return count.bit_length() - 1


def column_cuts(features):
    ends = [features * sum(PIECES[: c + 1]) // sum(PIECES) for c in range(CHUNKS)]
    return list(zip([0] + ends[:-1], ends))


def spare_width(axis_width):
    return -(-2 * axis_width // LANES) * LANES


def slice_orders(axis_width):
    groups = axis_width // ATT_TP
    first = [groups << step for step in range(bits_of(ATT_TP))]
    second = [first[1], first[0], *first[2:]]
    return first, second


def exchange(block, route):
    count = lax.axis_size("wide")
    return lax.ppermute(block, "wide", [(i, route(i)) for i in range(count)])


def on_odd_chip():
    index = lax.axis_index("wide") // (lax.axis_size("wide") // ATT_TP)
    odd = 0
    for step in range(bits_of(ATT_TP)):
        odd ^= index >> step & 1
    return odd == 1


class Routes:
    def __init__(self, axis_width):
        groups = axis_width // ATT_TP
        orders = slice_orders(axis_width)
        odd = lambda i: (i // groups).bit_count() & 1
        self.pair = lambda i: i ^ 1
        self.steps = [
            lambda i, step=step: i ^ orders[(i & 1) ^ odd(i)][step] ^ 1
            for step in range(bits_of(ATT_TP))
        ]
        self.last = lambda i: i ^ orders[(i & 1) ^ odd(i)][-1] ^ odd(i)
        self.groups = [lambda i, k=k: i ^ 1 << k for k in range(1, bits_of(groups))]


def relative_masks(order):
    steps = len(order)
    masks = []
    for j in range(1 << steps):
        mask = 0
        for step in range(steps):
            if j >> (steps - 1 - step) & 1:
                mask ^= order[step]
        masks.append(mask)
    return masks


def started(sources, targets, sems):
    copies = [
        pltpu.make_async_copy(source, target, sems.at[n])
        for n, (source, target) in enumerate(zip(sources, targets))
    ]
    for copy in copies:
        copy.start()
    return copies


def attend_kernel(axis_width, *refs):
    sources, (ordered, w_out), scratch = refs[:9], refs[9:11], refs[11:]
    *inputs, attended, sems = scratch
    copies = started(sources, [*inputs, w_out], sems)
    parents, table, lengths, expert_ids, gate_weights, queries, tree_kv, kv_cache = inputs
    seq_count, node_count = parents.shape
    head_dim = tree_kv.shape[-1]
    head_count = queries.shape[1] // head_dim
    pages = table.shape[1]
    cached = pages * kv_cache.shape[2]
    all_nodes = seq_count * node_count
    query_count = head_count * node_count
    f32, bf16 = jnp.float32, jnp.bfloat16

    copies[0].wait()
    lane = lax.broadcasted_iota(jnp.int32, (8, all_nodes), 1)
    shifted = [
        jnp.where(parents[s : s + 1, :] >= 0, parents[s : s + 1, :] + s * node_count, -1)
        for s in range(seq_count)
    ]
    above = jnp.broadcast_to(jnp.concatenate(shifted, axis=1), lane.shape)
    above = jnp.where(above >= 0, above, lane)
    words = jnp.left_shift(1, lane % node_count)
    for repeat in range(max(node_count - 1, 1).bit_length()):
        if repeat:
            above = jnp.take_along_axis(above, above, axis=1)
        words = words | jnp.take_along_axis(words, above, axis=1)

    for copy in copies[1:-1]:
        copy.wait()
    query_nodes = lax.broadcasted_iota(jnp.int32, (8, query_count), 1) % node_count
    node_rows = lax.broadcasted_iota(jnp.int32, (node_count, query_count), 0)
    positions = lax.broadcasted_iota(jnp.int32, (cached, query_count), 0)
    for s in range(seq_count):
        own = slice(s * node_count, (s + 1) * node_count)
        word = jnp.take_along_axis(words, query_nodes + s * node_count, axis=1)
        word = jnp.broadcast_to(word[:1], node_rows.shape)
        tree_open = (lax.shift_right_logical(word, node_rows) & 1) == 1
        keys = [kv_cache[0, table[s, p]] for p in range(pages)]
        values = [kv_cache[1, table[s, p]] for p in range(pages)]
        key_rows = jnp.concatenate(keys + [tree_kv[0, own]], axis=0)
        value_rows = jnp.concatenate(values + [tree_kv[1, own]], axis=0)
        query_rows = jnp.concatenate(
            [queries[own, h * head_dim : (h + 1) * head_dim] for h in range(head_count)], axis=0
        )
        scores = lax.dot_general(
            key_rows, query_rows, (((1,), (1,)), ((), ())), preferred_element_type=f32
        ) * head_dim ** (-0.5)
        cache_scores = jnp.where(positions < lengths[0, s], scores[:cached], -jnp.inf)
        tree_scores = jnp.where(tree_open, scores[cached:], -jnp.inf)
        masked = jnp.concatenate([cache_scores, tree_scores], axis=0)
        highest = jnp.max(masked, axis=0, keepdims=True)
        probs = jnp.exp(masked - highest)
        total = jnp.broadcast_to(jnp.sum(probs, axis=0, keepdims=True), (head_dim, query_count))
        blended = lax.dot_general(
            probs.astype(bf16), value_rows, (((0,), (0,)), ((), ())), preferred_element_type=f32
        )
        blended = (blended / total.T).astype(bf16)
        for h in range(head_count):
            attended[own, h * head_dim : (h + 1) * head_dim] = blended[
                h * node_count : (h + 1) * node_count
            ]

    listed, row_count = expert_ids.shape
    spread_width = spare_width(axis_width)
    expert = lax.broadcasted_iota(jnp.int32, (spread_width, row_count), 0)
    weight = jnp.zeros((spread_width, row_count), f32)
    for k in range(listed):
        weight += jnp.where(
            expert_ids[k : k + 1, :] == expert % axis_width, gate_weights[k : k + 1, :], 0.0
        )
    upper = weight.astype(bf16).astype(f32)
    parts = jnp.where(
        expert < axis_width, upper, jnp.where(expert < 2 * axis_width, weight - upper, 0.0)
    )
    ordered[:row_count, -spread_width:] = parts.T.astype(bf16)
    rest = (all_nodes - row_count, spread_width)
    ordered[row_count:, -spread_width:] = jnp.zeros(rest, bf16)

    device = lax.axis_index("wide")
    groups = axis_width // ATT_TP
    first, second = [relative_masks(order) for order in slice_orders(axis_width)]
    block = all_nodes // ATT_TP
    picked = []
    for one, other in zip(first, second):
        target = (device ^ jnp.where(device & 1 == 0, one, other)) // groups
        picked.append(attended[pl.ds(pl.multiple_of(target * block, block), block), :])
    ordered[:, : queries.shape[1]] = jnp.concatenate(picked, axis=0)
    copies[-1].wait()


def project_kernel(own_rows, cut, own, other, w_out, kept, sent, *extra):
    rows = jnp.where(on_odd_chip(), other[...], own[...])
    width = w_out.shape[0]
    if extra:
        extra[0][...] = rows[: 2 * own_rows, width:]
    half = rows.shape[0] // 2
    projected = jnp.dot(
        rows[:, :width], w_out[:, cut[0] : cut[1]], preferred_element_type=jnp.float32
    )
    kept[...] = projected[:half]
    sent[...] = projected[half:].astype(jnp.bfloat16)


def project(own, other, w_out, own_rows):
    spare = spare_width(lax.axis_size("wide"))
    halves = []
    for c, cut in enumerate(column_cuts(w_out.shape[1])):
        shapes = kept_and_sent(own.shape[0], [cut])
        last = c == CHUNKS - 1
        halves += local_call(
            functools.partial(project_kernel, own_rows, cut),
            "project",
            shapes + [pltpu.VMEM((2 * own_rows, spare), jnp.bfloat16)] * last,
            [own, other, w_out],
            flops=HINT * c,
        )
    return halves


def kept_and_sent(rows, cuts):
    shapes = []
    for low, high in cuts:
        shapes.append(pltpu.VMEM((rows // 2, high - low), jnp.float32))
        shapes.append(pltpu.VMEM((rows // 2, high - low), jnp.bfloat16))
    return shapes


def attend(
    queries, tree_kv, kv_cache, table, lengths, parents, w_out, expert_ids, gate_weights
):
    axis_width = lax.axis_size("wide")
    rows, width = queries.shape
    given = [parents, table, lengths, expert_ids.T, gate_weights.T, queries, tree_kv, kv_cache, w_out]
    spaces = [pltpu.VMEM, pltpu.SMEM, pltpu.SMEM] + [pltpu.VMEM] * 5
    given = [pltpu.with_memory_space_constraint(x, pltpu.HBM) for x in given]
    return pl.pallas_call(
        functools.partial(attend_kernel, axis_width),
        out_shape=[
            pltpu.VMEM((rows, width + spare_width(axis_width)), jnp.bfloat16),
            pltpu.VMEM(w_out.shape, w_out.dtype),
        ],
        in_specs=[pl.BlockSpec(memory_space=pltpu.HBM)] * len(given),
        out_specs=[pl.BlockSpec(memory_space=pltpu.VMEM)] * 2,
        scratch_shapes=[space(x.shape, x.dtype) for space, x in zip(spaces, given)]
        + [pltpu.VMEM(queries.shape, jnp.bfloat16), pltpu.SemaphoreType.DMA((len(given),))],
        compiler_params=pltpu.CompilerParams(vmem_limit_bytes=16 * 1024 * 1024),
        name="attend",
    )(*given)


def feed_kernel(cut, tile, pairs, first, *refs):
    hidden, weights, refs = refs[:2], refs[2 : 2 + pairs], refs[2 + pairs :]
    before, after = (None, refs) if first else (refs[:pairs], refs[pairs:])
    rows = jnp.concatenate([half[:, : cut[1] - cut[0]] for half in hidden], axis=0)
    for m in range(pairs):
        for n in range(weights[m].shape[2] // tile):
            columns = slice(n * tile, (n + 1) * tile)
            share = jnp.dot(
                rows, weights[m][0, cut[0] : cut[1], columns], preferred_element_type=jnp.float32
            )
            after[m][:, columns] = share if first else before[m][:, columns] + share


def finish_kernel(axis_width, spare, cut, out_cut, tile, owners, *refs):
    count = len(owners)
    hidden, carrier, refs = refs[:2], refs[2:4], refs[4:]
    feeds, downs, sums = refs[: 2 * count], refs[2 * count : 3 * count], refs[3 * count : 5 * count]
    kept, sent = refs[5 * count : 5 * count + 2]
    activated, row_weight = refs[5 * count + 2 : 6 * count + 2], refs[6 * count + 2 :]
    f32, bf16 = jnp.float32, jnp.bfloat16
    width = cut[1] - cut[0]
    device = lax.axis_index("wide")
    rows = jnp.concatenate([half[:, :width] for half in hidden], axis=0)
    parts = jnp.concatenate([half[:, -spare:] for half in carrier], axis=0)
    lane = lax.broadcasted_iota(jnp.int32, parts.shape, 1)
    piece = slice(*cut)
    for m, owner in enumerate(owners):
        expert = device ^ owner
        mine = (lane == expert) | (lane == expert + axis_width)
        row_weight[m][...] = jnp.sum(jnp.where(mine, parts.astype(f32), 0.0), axis=1, keepdims=True)
        for n in range(feeds[2 * m].shape[2] // tile):
            columns = slice(n * tile, (n + 1) * tile)
            gate_part, up_part = [
                sums[2 * m + k][:, columns]
                + jnp.dot(rows, feeds[2 * m + k][0, piece, columns], preferred_element_type=f32)
                for k in range(2)
            ]
            activated[m][:, columns] = (
                gate_part / (1.0 + jnp.exp(-gate_part)) * up_part
            ).astype(bf16)
    produce(activated, downs, row_weight, out_cut, kept, sent, tile)


def down_kernel(cut, tile, count, *refs):
    activated, row_weight, downs = [refs[k * count : (k + 1) * count] for k in range(3)]
    produce(activated, downs, row_weight, cut, *refs[3 * count :], tile)


def produce(activated, downs, row_weight, cut, kept, sent, tile):
    half, width = kept.shape
    for start in range(0, width, tile):
        size = min(tile, width - start)
        columns = slice(cut[0] + start, cut[0] + start + size)
        weighted = 0.0
        for rows, w_down, weight in zip(activated, downs, row_weight):
            weighted += (
                jnp.dot(rows[...], w_down[0, :, columns], preferred_element_type=jnp.float32)
                * weight[...]
            )
        kept[:, start : start + size] = weighted[:half]
        sent[:, start : start + size] = weighted[half:].astype(jnp.bfloat16)


def local_call(kernel, name, out_shape, given, flops=0):
    return pl.pallas_call(
        kernel,
        out_shape=out_shape,
        in_specs=[pl.BlockSpec(memory_space=pltpu.VMEM)] * len(given),
        out_specs=[pl.BlockSpec(memory_space=pltpu.VMEM)] * len(out_shape),
        compiler_params=pltpu.CompilerParams(vmem_limit_bytes=16 * 1024 * 1024),
        cost_estimate=pl.CostEstimate(flops=flops, bytes_accessed=0, transcendentals=0) if flops else None,
        name=name,
    )(*given)


def experts(hidden, owners, feeds, downs):
    axis_width = lax.axis_size("wide")
    rows = 2 * hidden[0][0].shape[0]
    hidden_width, features = downs[0].shape[1:]
    cuts = column_cuts(features)
    spare = spare_width(axis_width)
    count = len(owners)
    tile = 256 if hidden_width % 256 == 0 else LANES
    wide = pltpu.VMEM((rows, hidden_width), jnp.float32)
    sums = []
    for c in range(CHUNKS - 1):
        kernel = functools.partial(feed_kernel, cuts[c], tile, 2 * count, c == 0)
        sums = local_call(kernel, "feed", [wide] * (2 * count), [*hidden[c], *feeds, *sums])
    kept, sent, *rest = local_call(
        functools.partial(finish_kernel, axis_width, spare, cuts[-1], cuts[0], tile, owners),
        "finish",
        kept_and_sent(rows, cuts[:1])
        + [pltpu.VMEM((rows, hidden_width), jnp.bfloat16)] * count
        + [pltpu.VMEM((rows, 1), jnp.float32)] * count,
        [*hidden[-1], *hidden[CARRIER], *feeds, *downs, *sums],
    )
    produced = [(kept, sent)]
    for c in range(1, CHUNKS):
        kernel = functools.partial(down_kernel, cuts[c], tile, count)
        shapes = kept_and_sent(rows, cuts[c : c + 1])
        produced.append(local_call(kernel, "down", shapes, [*rest, *downs]))
    return produced


def halved(block):
    half = block.shape[0] // 2
    return block[:half], block[half:].astype(jnp.bfloat16)


def ordered_after(value, earlier):
    return value if earlier is None else lax.optimization_barrier((value, earlier))[0]


def reduce_and_gather(halves, extra, routes):
    f32, bf16 = jnp.float32, jnp.bfloat16
    parts = [list(halves[2 * c : 2 * c + 2]) for c in range(CHUNKS)]
    for number, route in enumerate(routes.steps[:-1]):
        earlier = None
        for c, part in enumerate(parts):
            kept, sent = part
            kept = kept + ordered_after(exchange(sent, route), earlier).astype(f32)
            if number < len(routes.steps) - 2:
                part[:] = halved(kept)
            else:
                if c == CARRIER:
                    kept = jnp.concatenate([kept, extra.astype(f32)], axis=1)
                part[:] = kept, kept.astype(bf16)
            earlier = part[1]
    blocks, earlier = [], None
    for kept, sent in parts:
        half = kept.shape[0] // 2
        other = ordered_after(exchange(sent, routes.steps[-1]), earlier).astype(f32)
        blocks.append((kept + jnp.concatenate([other[half:], other[:half]], axis=0)).astype(bf16))
        earlier = blocks[-1]
    gathers = routes.steps[-2::-1] + routes.groups
    for route in gathers[:-1]:
        earlier = None
        for c, block in enumerate(blocks):
            other = ordered_after(exchange(block, route), earlier)
            blocks[c] = earlier = jnp.concatenate([block, other], axis=0)
    return [(block, exchange(block, gathers[-1])) for block in blocks]


def body(
    queries,
    tree_kv,
    kv_cache,
    block_table,
    cache_lengths,
    parents,
    w_out,
    w_gate,
    w_up,
    w_down,
    expert_ids,
    gate_weights,
):
    axis_width = lax.axis_size("wide")
    routes = Routes(axis_width)
    owners = (0, 1)
    own, fetched = attend(
        queries, tree_kv, kv_cache, block_table, cache_lengths, parents, w_out, expert_ids,
        gate_weights,
    )
    *halves, extra = project(own, exchange(own, routes.pair), fetched, expert_ids.shape[0])
    others = [exchange(x, routes.pair) for x in (w_gate, w_up, w_down)]
    feeds = [w_gate, w_up, *others[:2]]
    downs = [w_down, others[2]]
    hidden = reduce_and_gather(halves, extra, routes)
    parts = [list(pair) for pair in experts(hidden, owners, feeds, downs)]
    for route in routes.groups[::-1] + routes.steps[:-1]:
        earlier = None
        for part in parts:
            kept, sent = part
            other = ordered_after(exchange(sent, route), earlier)
            part[:] = halved(kept + other.astype(jnp.float32))
            earlier = part[1]
    results, earlier = [], None
    for kept, sent in parts:
        other = ordered_after(exchange(sent, routes.steps[-1]), earlier).astype(jnp.float32)
        results.append((kept + other).astype(jnp.bfloat16))
        earlier = results[-1]
    result = jnp.concatenate(results, axis=1)
    return jnp.where(on_odd_chip(), exchange(result, routes.pair), result)


def solution(mesh):
    placed = (
        P(("groups", "wide"), None),
        P(None, ("groups", "wide"), None),
        P(None, ("groups", "wide"), None, None),
        P(("groups", "wide"), None),
        P(("groups", "wide"), None),
        P(("groups", "wide"), None),
        P("wide", None),
        P("wide", None, None),
        P("wide", None, None),
        P("wide", None, None),
        P(("groups", "wide"), None),
        P(("groups", "wide"), None),
    )
    return jax.shard_map(
        body, mesh=mesh, in_specs=placed, out_specs=P(("groups", "wide"), None), check_vma=False
    )
```

```python
import functools

import jax
import jax.numpy as jnp
from jax import lax
from jax.experimental import pallas as pl
from jax.experimental.pallas import tpu as pltpu
from jax.sharding import PartitionSpec as P

ATT_TP = 8
PIECES = (8, 8)
CHUNKS = len(PIECES)
CARRIER = 0
LANES = 128
HINT = 30_000_000_000


def bits_of(count):
    return count.bit_length() - 1


def column_cuts(features):
    ends = [features * sum(PIECES[: c + 1]) // sum(PIECES) for c in range(CHUNKS)]
    return list(zip([0] + ends[:-1], ends))


def spare_width(axis_width):
    return -(-2 * axis_width // LANES) * LANES


def slice_orders(axis_width):
    groups = axis_width // ATT_TP
    first = [groups << step for step in range(bits_of(ATT_TP))]
    return [*first[1:], first[0]], first


def return_orders(axis_width):
    second, first = slice_orders(axis_width)
    return [second[0], second[-1], *second[1:-1]], first


def exchange(block, route):
    count = lax.axis_size("wide")
    return lax.ppermute(block, "wide", [(i, route(i)) for i in range(count)])


def on_odd_chip():
    index = lax.axis_index("wide") // (lax.axis_size("wide") // ATT_TP)
    odd = 0
    for step in range(bits_of(ATT_TP)):
        odd ^= index >> step & 1
    return odd == 1


class Routes:
    def __init__(self, axis_width):
        groups = axis_width // ATT_TP
        orders = slice_orders(axis_width)
        odd = lambda i: (i // groups).bit_count() & 1
        self.pair = lambda i: i ^ 1
        steps = range(bits_of(ATT_TP))
        self.steps, self.returns = [
            [lambda i, order=order, k=k: i ^ order[(i & 1) ^ odd(i)][k] ^ 1 for k in steps]
            for order in (orders, return_orders(axis_width))
        ]
        self.groups = [lambda i, k=k: i ^ 1 << k for k in range(1, bits_of(groups))]


def relative_masks(order):
    steps = len(order)
    masks = []
    for j in range(1 << steps):
        mask = 0
        for step in range(steps):
            if j >> (steps - 1 - step) & 1:
                mask ^= order[step]
        masks.append(mask)
    return masks


def started(sources, targets, sems):
    copies = [
        pltpu.make_async_copy(source, target, sems.at[n])
        for n, (source, target) in enumerate(zip(sources, targets))
    ]
    for copy in copies:
        copy.start()
    return copies


def attend_kernel(axis_width, *refs):
    sources, (ordered, w_out), scratch = refs[:9], refs[9:11], refs[11:]
    *inputs, attended, sems = scratch
    copies = started(sources, [*inputs, w_out], sems)
    parents, table, lengths, expert_ids, gate_weights, queries, tree_kv, kv_cache = inputs
    seq_count, node_count = parents.shape
    head_dim = tree_kv.shape[-1]
    head_count = queries.shape[1] // head_dim
    pages = table.shape[1]
    cached = pages * kv_cache.shape[2]
    all_nodes = seq_count * node_count
    query_count = head_count * node_count
    f32, bf16 = jnp.float32, jnp.bfloat16

    copies[0].wait()
    lane = lax.broadcasted_iota(jnp.int32, (8, all_nodes), 1)
    shifted = [
        jnp.where(parents[s : s + 1, :] >= 0, parents[s : s + 1, :] + s * node_count, -1)
        for s in range(seq_count)
    ]
    above = jnp.broadcast_to(jnp.concatenate(shifted, axis=1), lane.shape)
    above = jnp.where(above >= 0, above, lane)
    words = jnp.left_shift(1, lane % node_count)
    for repeat in range(max(node_count - 1, 1).bit_length()):
        if repeat:
            above = jnp.take_along_axis(above, above, axis=1)
        words = words | jnp.take_along_axis(words, above, axis=1)

    for copy in copies[1:-1]:
        copy.wait()
    query_nodes = lax.broadcasted_iota(jnp.int32, (8, query_count), 1) % node_count
    node_rows = lax.broadcasted_iota(jnp.int32, (node_count, query_count), 0)
    positions = lax.broadcasted_iota(jnp.int32, (cached, query_count), 0)
    for s in range(seq_count):
        own = slice(s * node_count, (s + 1) * node_count)
        word = jnp.take_along_axis(words, query_nodes + s * node_count, axis=1)
        word = jnp.broadcast_to(word[:1], node_rows.shape)
        tree_open = (lax.shift_right_logical(word, node_rows) & 1) == 1
        keys = [kv_cache[0, table[s, p]] for p in range(pages)]
        values = [kv_cache[1, table[s, p]] for p in range(pages)]
        key_rows = jnp.concatenate(keys + [tree_kv[0, own]], axis=0)
        value_rows = jnp.concatenate(values + [tree_kv[1, own]], axis=0)
        query_rows = jnp.concatenate(
            [queries[own, h * head_dim : (h + 1) * head_dim] for h in range(head_count)], axis=0
        )
        scores = lax.dot_general(
            key_rows, query_rows, (((1,), (1,)), ((), ())), preferred_element_type=f32
        ) * head_dim ** (-0.5)
        cache_scores = jnp.where(positions < lengths[0, s], scores[:cached], -jnp.inf)
        tree_scores = jnp.where(tree_open, scores[cached:], -jnp.inf)
        masked = jnp.concatenate([cache_scores, tree_scores], axis=0)
        highest = jnp.max(masked, axis=0, keepdims=True)
        probs = jnp.exp(masked - highest)
        total = jnp.broadcast_to(jnp.sum(probs, axis=0, keepdims=True), (head_dim, query_count))
        blended = lax.dot_general(
            probs.astype(bf16), value_rows, (((0,), (0,)), ((), ())), preferred_element_type=f32
        )
        blended = (blended / total.T).astype(bf16)
        for h in range(head_count):
            attended[own, h * head_dim : (h + 1) * head_dim] = blended[
                h * node_count : (h + 1) * node_count
            ]

    listed, row_count = expert_ids.shape
    spread_width = spare_width(axis_width)
    expert = lax.broadcasted_iota(jnp.int32, (spread_width, row_count), 0)
    weight = jnp.zeros((spread_width, row_count), f32)
    for k in range(listed):
        weight += jnp.where(
            expert_ids[k : k + 1, :] == expert % axis_width, gate_weights[k : k + 1, :], 0.0
        )
    upper = weight.astype(bf16).astype(f32)
    parts = jnp.where(
        expert < axis_width, upper, jnp.where(expert < 2 * axis_width, weight - upper, 0.0)
    )
    ordered[:row_count, -spread_width:] = parts.T.astype(bf16)
    rest = (all_nodes - row_count, spread_width)
    ordered[row_count:, -spread_width:] = jnp.zeros(rest, bf16)

    device = lax.axis_index("wide")
    groups = axis_width // ATT_TP
    first, second = [relative_masks(order) for order in slice_orders(axis_width)]
    block = all_nodes // ATT_TP
    picked = []
    for one, other in zip(first, second):
        target = (device ^ jnp.where(device & 1 == 0, one, other)) // groups
        picked.append(attended[pl.ds(pl.multiple_of(target * block, block), block), :])
    ordered[:, : queries.shape[1]] = jnp.concatenate(picked, axis=0)
    copies[-1].wait()


def project_kernel(own_rows, cut, own, other, w_out, kept, sent, *extra):
    rows = jnp.where(on_odd_chip(), other[...], own[...])
    width = w_out.shape[0]
    if extra:
        extra[0][...] = rows[: 2 * own_rows, width:]
    half = rows.shape[0] // 2
    projected = jnp.dot(
        rows[:, :width], w_out[:, cut[0] : cut[1]], preferred_element_type=jnp.float32
    )
    kept[...] = projected[:half]
    sent[...] = projected[half:].astype(jnp.bfloat16)


def project(own, other, w_out, own_rows):
    spare = spare_width(lax.axis_size("wide"))
    halves = []
    for c, cut in enumerate(column_cuts(w_out.shape[1])):
        shapes = kept_and_sent(own.shape[0], [cut])
        last = c == CHUNKS - 1
        halves += local_call(
            functools.partial(project_kernel, own_rows, cut),
            "project",
            shapes + [pltpu.VMEM((2 * own_rows, spare), jnp.bfloat16)] * last,
            [own, other, w_out],
            flops=HINT * c,
        )
    return halves


def kept_and_sent(rows, cuts):
    shapes = []
    for low, high in cuts:
        shapes.append(pltpu.VMEM((rows // 2, high - low), jnp.float32))
        shapes.append(pltpu.VMEM((rows // 2, high - low), jnp.bfloat16))
    return shapes


def attend(
    queries, tree_kv, kv_cache, table, lengths, parents, w_out, expert_ids, gate_weights
):
    axis_width = lax.axis_size("wide")
    rows, width = queries.shape
    given = [parents, table, lengths, expert_ids.T, gate_weights.T, queries, tree_kv, kv_cache, w_out]
    spaces = [pltpu.VMEM, pltpu.SMEM, pltpu.SMEM] + [pltpu.VMEM] * 5
    given = [pltpu.with_memory_space_constraint(x, pltpu.HBM) for x in given]
    return pl.pallas_call(
        functools.partial(attend_kernel, axis_width),
        out_shape=[
            pltpu.VMEM((rows, width + spare_width(axis_width)), jnp.bfloat16),
            pltpu.VMEM(w_out.shape, w_out.dtype),
        ],
        in_specs=[pl.BlockSpec(memory_space=pltpu.HBM)] * len(given),
        out_specs=[pl.BlockSpec(memory_space=pltpu.VMEM)] * 2,
        scratch_shapes=[space(x.shape, x.dtype) for space, x in zip(spaces, given)]
        + [pltpu.VMEM(queries.shape, jnp.bfloat16), pltpu.SemaphoreType.DMA((len(given),))],
        compiler_params=pltpu.CompilerParams(vmem_limit_bytes=16 * 1024 * 1024),
        name="attend",
    )(*given)


def arranged(halves, columns, axis_width):
    rows = jnp.concatenate([half[:, columns] for half in halves], axis=0)
    groups = axis_width // ATT_TP
    block = rows.shape[0] // (groups // 2 * ATT_TP)
    results = []
    for order, other in zip(slice_orders(axis_width), return_orders(axis_width)):
        masks = relative_masks(order)
        places = [masks.index(mask) for mask in relative_masks(other)]
        starts = [(k * ATT_TP + place) * block for k in range(groups // 2) for place in places]
        results.append(jnp.concatenate([rows[x : x + block] for x in starts], axis=0))
    role = (lax.axis_index("wide") & 1) ^ on_odd_chip().astype(jnp.int32)
    return jnp.where(role == 0, results[0], results[1])


def feed_kernel(axis_width, cut, tile, pairs, first, *refs):
    hidden, weights, refs = refs[:2], refs[2 : 2 + pairs], refs[2 + pairs :]
    before, after = (None, refs) if first else (refs[:pairs], refs[pairs:])
    rows = arranged(hidden, slice(0, cut[1] - cut[0]), axis_width)
    for m in range(pairs):
        for n in range(weights[m].shape[2] // tile):
            columns = slice(n * tile, (n + 1) * tile)
            share = jnp.dot(
                rows, weights[m][0, cut[0] : cut[1], columns], preferred_element_type=jnp.float32
            )
            after[m][:, columns] = share if first else before[m][:, columns] + share


def finish_kernel(axis_width, spare, cut, out_cut, tile, owners, *refs):
    count = len(owners)
    hidden, carrier, refs = refs[:2], refs[2:4], refs[4:]
    feeds, downs, sums = refs[: 2 * count], refs[2 * count : 3 * count], refs[3 * count : 5 * count]
    kept, sent = refs[5 * count : 5 * count + 2]
    activated, row_weight = refs[5 * count + 2 : 6 * count + 2], refs[6 * count + 2 :]
    f32, bf16 = jnp.float32, jnp.bfloat16
    width = cut[1] - cut[0]
    device = lax.axis_index("wide")
    rows = arranged(hidden, slice(0, width), axis_width)
    parts = arranged(carrier, slice(-spare, None), axis_width)
    lane = lax.broadcasted_iota(jnp.int32, parts.shape, 1)
    piece = slice(*cut)
    for m, owner in enumerate(owners):
        expert = device ^ owner
        mine = (lane == expert) | (lane == expert + axis_width)
        row_weight[m][...] = jnp.sum(jnp.where(mine, parts.astype(f32), 0.0), axis=1, keepdims=True)
        for n in range(feeds[2 * m].shape[2] // tile):
            columns = slice(n * tile, (n + 1) * tile)
            gate_part, up_part = [
                sums[2 * m + k][:, columns]
                + jnp.dot(rows, feeds[2 * m + k][0, piece, columns], preferred_element_type=f32)
                for k in range(2)
            ]
            activated[m][:, columns] = (
                gate_part / (1.0 + jnp.exp(-gate_part)) * up_part
            ).astype(bf16)
    produce(activated, downs, row_weight, out_cut, kept, sent, tile)


def down_kernel(cut, tile, count, *refs):
    activated, row_weight, downs = [refs[k * count : (k + 1) * count] for k in range(3)]
    produce(activated, downs, row_weight, cut, *refs[3 * count :], tile)


def produce(activated, downs, row_weight, cut, kept, sent, tile):
    half, width = kept.shape
    for start in range(0, width, tile):
        size = min(tile, width - start)
        columns = slice(cut[0] + start, cut[0] + start + size)
        weighted = 0.0
        for rows, w_down, weight in zip(activated, downs, row_weight):
            weighted += (
                jnp.dot(rows[...], w_down[0, :, columns], preferred_element_type=jnp.float32)
                * weight[...]
            )
        kept[:, start : start + size] = weighted[:half]
        sent[:, start : start + size] = weighted[half:].astype(jnp.bfloat16)


def local_call(kernel, name, out_shape, given, flops=0):
    return pl.pallas_call(
        kernel,
        out_shape=out_shape,
        in_specs=[pl.BlockSpec(memory_space=pltpu.VMEM)] * len(given),
        out_specs=[pl.BlockSpec(memory_space=pltpu.VMEM)] * len(out_shape),
        compiler_params=pltpu.CompilerParams(vmem_limit_bytes=16 * 1024 * 1024),
        cost_estimate=pl.CostEstimate(flops=flops, bytes_accessed=0, transcendentals=0) if flops else None,
        name=name,
    )(*given)


def experts(hidden, owners, feeds, downs):
    axis_width = lax.axis_size("wide")
    rows = 2 * hidden[0][0].shape[0]
    hidden_width, features = downs[0].shape[1:]
    cuts = column_cuts(features)
    spare = spare_width(axis_width)
    count = len(owners)
    tile = 256 if hidden_width % 256 == 0 else LANES
    wide = pltpu.VMEM((rows, hidden_width), jnp.float32)
    sums = []
    for c in range(CHUNKS - 1):
        kernel = functools.partial(feed_kernel, axis_width, cuts[c], tile, 2 * count, c == 0)
        sums = local_call(kernel, "feed", [wide] * (2 * count), [*hidden[c], *feeds, *sums])
    kept, sent, *rest = local_call(
        functools.partial(finish_kernel, axis_width, spare, cuts[-1], cuts[0], tile, owners),
        "finish",
        kept_and_sent(rows, cuts[:1])
        + [pltpu.VMEM((rows, hidden_width), jnp.bfloat16)] * count
        + [pltpu.VMEM((rows, 1), jnp.float32)] * count,
        [*hidden[-1], *hidden[CARRIER], *feeds, *downs, *sums],
    )
    produced = [(kept, sent)]
    for c in range(1, CHUNKS):
        kernel = functools.partial(down_kernel, cuts[c], tile, count)
        shapes = kept_and_sent(rows, cuts[c : c + 1])
        produced.append(local_call(kernel, "down", shapes, [*rest, *downs]))
    return produced


def halved(block):
    half = block.shape[0] // 2
    return block[:half], block[half:].astype(jnp.bfloat16)


def ordered_after(value, earlier):
    return value if earlier is None else lax.optimization_barrier((value, earlier))[0]


def reduce_and_gather(halves, extra, routes):
    f32, bf16 = jnp.float32, jnp.bfloat16
    parts = [list(halves[2 * c : 2 * c + 2]) for c in range(CHUNKS)]
    for number, route in enumerate(routes.steps[:-1]):
        earlier = None
        for c, part in enumerate(parts):
            kept, sent = part
            kept = kept + ordered_after(exchange(sent, route), earlier).astype(f32)
            if number < len(routes.steps) - 2:
                part[:] = halved(kept)
            else:
                if c == CARRIER:
                    kept = jnp.concatenate([kept, extra.astype(f32)], axis=1)
                part[:] = kept, kept.astype(bf16)
            earlier = part[1]
    blocks, earlier = [], None
    for kept, sent in parts:
        half = kept.shape[0] // 2
        other = ordered_after(exchange(sent, routes.steps[-1]), earlier).astype(f32)
        blocks.append((kept + jnp.concatenate([other[half:], other[:half]], axis=0)).astype(bf16))
        earlier = blocks[-1]
    gathers = routes.steps[-2::-1] + routes.groups
    for route in gathers[:-1]:
        earlier = None
        for c, block in enumerate(blocks):
            other = ordered_after(exchange(block, route), earlier)
            blocks[c] = earlier = jnp.concatenate([block, other], axis=0)
    return [(block, exchange(block, gathers[-1])) for block in blocks]


def body(
    queries,
    tree_kv,
    kv_cache,
    block_table,
    cache_lengths,
    parents,
    w_out,
    w_gate,
    w_up,
    w_down,
    expert_ids,
    gate_weights,
):
    axis_width = lax.axis_size("wide")
    routes = Routes(axis_width)
    owners = (0, 1)
    own, fetched = attend(
        queries, tree_kv, kv_cache, block_table, cache_lengths, parents, w_out, expert_ids,
        gate_weights,
    )
    *halves, extra = project(own, exchange(own, routes.pair), fetched, expert_ids.shape[0])
    others = [exchange(x, routes.pair) for x in (w_gate, w_up, w_down)]
    feeds = [w_gate, w_up, *others[:2]]
    downs = [w_down, others[2]]
    hidden = reduce_and_gather(halves, extra, routes)
    parts = [list(pair) for pair in experts(hidden, owners, feeds, downs)]
    for route in routes.groups[::-1] + routes.returns[:-1]:
        earlier = None
        for part in parts:
            kept, sent = part
            other = ordered_after(exchange(sent, route), earlier)
            part[:] = halved(kept + other.astype(jnp.float32))
            earlier = part[1]
    results, earlier = [], None
    for kept, sent in parts:
        other = ordered_after(exchange(sent, routes.returns[-1]), earlier).astype(jnp.float32)
        results.append((kept + other).astype(jnp.bfloat16))
        earlier = results[-1]
    result = jnp.concatenate(results, axis=1)
    return jnp.where(on_odd_chip(), exchange(result, routes.pair), result)


def solution(mesh):
    placed = (
        P(("groups", "wide"), None),
        P(None, ("groups", "wide"), None),
        P(None, ("groups", "wide"), None, None),
        P(("groups", "wide"), None),
        P(("groups", "wide"), None),
        P(("groups", "wide"), None),
        P("wide", None),
        P("wide", None, None),
        P("wide", None, None),
        P("wide", None, None),
        P(("groups", "wide"), None),
        P(("groups", "wide"), None),
    )
    return jax.shard_map(
        body, mesh=mesh, in_specs=placed, out_specs=P(("groups", "wide"), None), check_vma=False
    )
```

```python
import functools

import jax
import jax.numpy as jnp
from jax import lax
from jax.experimental import pallas as pl
from jax.experimental.pallas import tpu as pltpu
from jax.sharding import PartitionSpec as P

ATT_TP = 8
PIECES = (8, 8)
CHUNKS = len(PIECES)
CARRIER = 0
LANES = 128
HINT = 30_000_000_000


def bits_of(count):
    return count.bit_length() - 1


def column_cuts(features):
    ends = [features * sum(PIECES[: c + 1]) // sum(PIECES) for c in range(CHUNKS)]
    return list(zip([0] + ends[:-1], ends))


def spare_width(axis_width):
    return -(-2 * axis_width // LANES) * LANES


def slice_orders(axis_width):
    low, *rest, high = [axis_width // ATT_TP << step for step in range(bits_of(ATT_TP))]
    return [*rest, high, low], [low, *rest, high]


def return_orders(axis_width):
    low, *rest, high = [axis_width // ATT_TP << step for step in range(bits_of(ATT_TP))]
    return [*rest, low, high], [low, high, *rest]


def exchange(block, route):
    count = lax.axis_size("wide")
    return lax.ppermute(block, "wide", [(i, route(i)) for i in range(count)])


def on_odd_chip():
    index = lax.axis_index("wide") // (lax.axis_size("wide") // ATT_TP)
    odd = 0
    for step in range(bits_of(ATT_TP)):
        odd ^= index >> step & 1
    return odd == 1


class Routes:
    def __init__(self, axis_width):
        groups = axis_width // ATT_TP
        orders = slice_orders(axis_width)
        odd = lambda i: (i // groups).bit_count() & 1
        self.pair = lambda i: i ^ 1
        steps = range(bits_of(ATT_TP))
        self.steps, self.returns = [
            [lambda i, order=order, k=k: i ^ order[(i & 1) ^ odd(i)][k] ^ 1 for k in steps]
            for order in (orders, return_orders(axis_width))
        ]
        self.groups = [lambda i, k=k: i ^ 1 << k for k in range(1, bits_of(groups))]


def relative_masks(order):
    steps = len(order)
    masks = []
    for j in range(1 << steps):
        mask = 0
        for step in range(steps):
            if j >> (steps - 1 - step) & 1:
                mask ^= order[step]
        masks.append(mask)
    return masks


def started(sources, targets, sems):
    copies = [
        pltpu.make_async_copy(source, target, sems.at[n])
        for n, (source, target) in enumerate(zip(sources, targets))
    ]
    for copy in copies:
        copy.start()
    return copies


def attend_kernel(axis_width, *refs):
    sources, (ordered, w_out), scratch = refs[:9], refs[9:11], refs[11:]
    *inputs, attended, sems = scratch
    copies = started(sources, [*inputs, w_out], sems)
    parents, table, lengths, expert_ids, gate_weights, queries, tree_kv, kv_cache = inputs
    seq_count, node_count = parents.shape
    head_dim = tree_kv.shape[-1]
    head_count = queries.shape[1] // head_dim
    pages = table.shape[1]
    cached = pages * kv_cache.shape[2]
    all_nodes = seq_count * node_count
    query_count = head_count * node_count
    f32, bf16 = jnp.float32, jnp.bfloat16

    copies[0].wait()
    lane = lax.broadcasted_iota(jnp.int32, (8, all_nodes), 1)
    shifted = [
        jnp.where(parents[s : s + 1, :] >= 0, parents[s : s + 1, :] + s * node_count, -1)
        for s in range(seq_count)
    ]
    above = jnp.broadcast_to(jnp.concatenate(shifted, axis=1), lane.shape)
    above = jnp.where(above >= 0, above, lane)
    words = jnp.left_shift(1, lane % node_count)
    for repeat in range(max(node_count - 1, 1).bit_length()):
        if repeat:
            above = jnp.take_along_axis(above, above, axis=1)
        words = words | jnp.take_along_axis(words, above, axis=1)

    for copy in copies[1:-1]:
        copy.wait()
    query_nodes = lax.broadcasted_iota(jnp.int32, (8, query_count), 1) % node_count
    node_rows = lax.broadcasted_iota(jnp.int32, (node_count, query_count), 0)
    positions = lax.broadcasted_iota(jnp.int32, (cached, query_count), 0)
    for s in range(seq_count):
        own = slice(s * node_count, (s + 1) * node_count)
        word = jnp.take_along_axis(words, query_nodes + s * node_count, axis=1)
        word = jnp.broadcast_to(word[:1], node_rows.shape)
        tree_open = (lax.shift_right_logical(word, node_rows) & 1) == 1
        keys = [kv_cache[0, table[s, p]] for p in range(pages)]
        values = [kv_cache[1, table[s, p]] for p in range(pages)]
        key_rows = jnp.concatenate(keys + [tree_kv[0, own]], axis=0)
        value_rows = jnp.concatenate(values + [tree_kv[1, own]], axis=0)
        query_rows = jnp.concatenate(
            [queries[own, h * head_dim : (h + 1) * head_dim] for h in range(head_count)], axis=0
        )
        scores = lax.dot_general(
            key_rows, query_rows, (((1,), (1,)), ((), ())), preferred_element_type=f32
        ) * head_dim ** (-0.5)
        cache_scores = jnp.where(positions < lengths[0, s], scores[:cached], -jnp.inf)
        tree_scores = jnp.where(tree_open, scores[cached:], -jnp.inf)
        masked = jnp.concatenate([cache_scores, tree_scores], axis=0)
        highest = jnp.max(masked, axis=0, keepdims=True)
        probs = jnp.exp(masked - highest)
        total = jnp.broadcast_to(jnp.sum(probs, axis=0, keepdims=True), (head_dim, query_count))
        blended = lax.dot_general(
            probs.astype(bf16), value_rows, (((0,), (0,)), ((), ())), preferred_element_type=f32
        )
        blended = (blended / total.T).astype(bf16)
        for h in range(head_count):
            attended[own, h * head_dim : (h + 1) * head_dim] = blended[
                h * node_count : (h + 1) * node_count
            ]

    listed, row_count = expert_ids.shape
    spread_width = spare_width(axis_width)
    expert = lax.broadcasted_iota(jnp.int32, (spread_width, row_count), 0)
    weight = jnp.zeros((spread_width, row_count), f32)
    for k in range(listed):
        weight += jnp.where(
            expert_ids[k : k + 1, :] == expert % axis_width, gate_weights[k : k + 1, :], 0.0
        )
    upper = weight.astype(bf16).astype(f32)
    parts = jnp.where(
        expert < axis_width, upper, jnp.where(expert < 2 * axis_width, weight - upper, 0.0)
    )
    ordered[:row_count, -spread_width:] = parts.T.astype(bf16)
    rest = (all_nodes - row_count, spread_width)
    ordered[row_count:, -spread_width:] = jnp.zeros(rest, bf16)

    device = lax.axis_index("wide")
    groups = axis_width // ATT_TP
    first, second = [relative_masks(order) for order in slice_orders(axis_width)]
    block = all_nodes // ATT_TP
    picked = []
    for one, other in zip(first, second):
        target = (device ^ jnp.where(device & 1 == 0, one, other)) // groups
        picked.append(attended[pl.ds(pl.multiple_of(target * block, block), block), :])
    ordered[:, : queries.shape[1]] = jnp.concatenate(picked, axis=0)
    copies[-1].wait()


def project_kernel(own_rows, cut, own, other, w_out, kept, sent, *extra):
    rows = jnp.where(on_odd_chip(), other[...], own[...])
    width = w_out.shape[0]
    if extra:
        extra[0][...] = rows[: 2 * own_rows, width:]
    half = rows.shape[0] // 2
    projected = jnp.dot(
        rows[:, :width], w_out[:, cut[0] : cut[1]], preferred_element_type=jnp.float32
    )
    kept[...] = projected[:half]
    sent[...] = projected[half:].astype(jnp.bfloat16)


def project(own, other, w_out, own_rows):
    spare = spare_width(lax.axis_size("wide"))
    halves = []
    for c, cut in enumerate(column_cuts(w_out.shape[1])):
        shapes = kept_and_sent(own.shape[0], [cut])
        last = c == CHUNKS - 1
        halves += local_call(
            functools.partial(project_kernel, own_rows, cut),
            "project",
            shapes + [pltpu.VMEM((2 * own_rows, spare), jnp.bfloat16)] * last,
            [own, other, w_out],
            flops=HINT * c,
        )
    return halves


def kept_and_sent(rows, cuts):
    shapes = []
    for low, high in cuts:
        shapes.append(pltpu.VMEM((rows // 2, high - low), jnp.float32))
        shapes.append(pltpu.VMEM((rows // 2, high - low), jnp.bfloat16))
    return shapes


def attend(
    queries, tree_kv, kv_cache, table, lengths, parents, w_out, expert_ids, gate_weights
):
    axis_width = lax.axis_size("wide")
    rows, width = queries.shape
    given = [parents, table, lengths, expert_ids.T, gate_weights.T, queries, tree_kv, kv_cache, w_out]
    spaces = [pltpu.VMEM, pltpu.SMEM, pltpu.SMEM] + [pltpu.VMEM] * 5
    given = [pltpu.with_memory_space_constraint(x, pltpu.HBM) for x in given]
    return pl.pallas_call(
        functools.partial(attend_kernel, axis_width),
        out_shape=[
            pltpu.VMEM((rows, width + spare_width(axis_width)), jnp.bfloat16),
            pltpu.VMEM(w_out.shape, w_out.dtype),
        ],
        in_specs=[pl.BlockSpec(memory_space=pltpu.HBM)] * len(given),
        out_specs=[pl.BlockSpec(memory_space=pltpu.VMEM)] * 2,
        scratch_shapes=[space(x.shape, x.dtype) for space, x in zip(spaces, given)]
        + [pltpu.VMEM(queries.shape, jnp.bfloat16), pltpu.SemaphoreType.DMA((len(given),))],
        compiler_params=pltpu.CompilerParams(vmem_limit_bytes=16 * 1024 * 1024),
        name="attend",
    )(*given)


def arranged(halves, columns, axis_width):
    rows = jnp.concatenate([half[:, columns] for half in halves], axis=0)
    groups = axis_width // ATT_TP
    block = rows.shape[0] // (groups // 2 * ATT_TP)
    results = []
    for order, other in zip(slice_orders(axis_width), return_orders(axis_width)):
        masks = relative_masks(order)
        places = [masks.index(mask) for mask in relative_masks(other)]
        starts = [(k * ATT_TP + place) * block for k in range(groups // 2) for place in places]
        results.append(jnp.concatenate([rows[x : x + block] for x in starts], axis=0))
    role = (lax.axis_index("wide") & 1) ^ on_odd_chip().astype(jnp.int32)
    return jnp.where(role == 0, results[0], results[1])


def feed_kernel(axis_width, cut, tile, pairs, first, *refs):
    hidden, weights, refs = refs[:2], refs[2 : 2 + pairs], refs[2 + pairs :]
    before, after = (None, refs) if first else (refs[:pairs], refs[pairs:])
    rows = arranged(hidden, slice(0, cut[1] - cut[0]), axis_width)
    for m in range(pairs):
        for n in range(weights[m].shape[2] // tile):
            columns = slice(n * tile, (n + 1) * tile)
            share = jnp.dot(
                rows, weights[m][0, cut[0] : cut[1], columns], preferred_element_type=jnp.float32
            )
            after[m][:, columns] = share if first else before[m][:, columns] + share


def finish_kernel(axis_width, spare, cut, out_cut, tile, owners, *refs):
    count = len(owners)
    hidden, carrier, refs = refs[:2], refs[2:4], refs[4:]
    feeds, downs, sums = refs[: 2 * count], refs[2 * count : 3 * count], refs[3 * count : 5 * count]
    kept, sent = refs[5 * count : 5 * count + 2]
    activated, row_weight = refs[5 * count + 2 : 6 * count + 2], refs[6 * count + 2 :]
    f32, bf16 = jnp.float32, jnp.bfloat16
    width = cut[1] - cut[0]
    device = lax.axis_index("wide")
    rows = arranged(hidden, slice(0, width), axis_width)
    parts = arranged(carrier, slice(-spare, None), axis_width)
    lane = lax.broadcasted_iota(jnp.int32, parts.shape, 1)
    piece = slice(*cut)
    for m, owner in enumerate(owners):
        expert = device ^ owner
        mine = (lane == expert) | (lane == expert + axis_width)
        row_weight[m][...] = jnp.sum(jnp.where(mine, parts.astype(f32), 0.0), axis=1, keepdims=True)
        for n in range(feeds[2 * m].shape[2] // tile):
            columns = slice(n * tile, (n + 1) * tile)
            gate_part, up_part = [
                sums[2 * m + k][:, columns]
                + jnp.dot(rows, feeds[2 * m + k][0, piece, columns], preferred_element_type=f32)
                for k in range(2)
            ]
            activated[m][:, columns] = (
                gate_part / (1.0 + jnp.exp(-gate_part)) * up_part
            ).astype(bf16)
    produce(activated, downs, row_weight, out_cut, kept, sent, tile)


def down_kernel(cut, tile, count, *refs):
    activated, row_weight, downs = [refs[k * count : (k + 1) * count] for k in range(3)]
    produce(activated, downs, row_weight, cut, *refs[3 * count :], tile)


def produce(activated, downs, row_weight, cut, kept, sent, tile):
    half, width = kept.shape
    for start in range(0, width, tile):
        size = min(tile, width - start)
        columns = slice(cut[0] + start, cut[0] + start + size)
        weighted = 0.0
        for rows, w_down, weight in zip(activated, downs, row_weight):
            weighted += (
                jnp.dot(rows[...], w_down[0, :, columns], preferred_element_type=jnp.float32)
                * weight[...]
            )
        kept[:, start : start + size] = weighted[:half]
        sent[:, start : start + size] = weighted[half:].astype(jnp.bfloat16)


def local_call(kernel, name, out_shape, given, flops=0):
    return pl.pallas_call(
        kernel,
        out_shape=out_shape,
        in_specs=[pl.BlockSpec(memory_space=pltpu.VMEM)] * len(given),
        out_specs=[pl.BlockSpec(memory_space=pltpu.VMEM)] * len(out_shape),
        compiler_params=pltpu.CompilerParams(vmem_limit_bytes=16 * 1024 * 1024),
        cost_estimate=pl.CostEstimate(flops=flops, bytes_accessed=0, transcendentals=0) if flops else None,
        name=name,
    )(*given)


def experts(hidden, owners, feeds, downs):
    axis_width = lax.axis_size("wide")
    rows = 2 * hidden[0][0].shape[0]
    hidden_width, features = downs[0].shape[1:]
    cuts = column_cuts(features)
    spare = spare_width(axis_width)
    count = len(owners)
    tile = 256 if hidden_width % 256 == 0 else LANES
    wide = pltpu.VMEM((rows, hidden_width), jnp.float32)
    sums = []
    for c in range(CHUNKS - 1):
        kernel = functools.partial(feed_kernel, axis_width, cuts[c], tile, 2 * count, c == 0)
        sums = local_call(kernel, "feed", [wide] * (2 * count), [*hidden[c], *feeds, *sums])
    kept, sent, *rest = local_call(
        functools.partial(finish_kernel, axis_width, spare, cuts[-1], cuts[0], tile, owners),
        "finish",
        kept_and_sent(rows, cuts[:1])
        + [pltpu.VMEM((rows, hidden_width), jnp.bfloat16)] * count
        + [pltpu.VMEM((rows, 1), jnp.float32)] * count,
        [*hidden[-1], *hidden[CARRIER], *feeds, *downs, *sums],
    )
    produced = [(kept, sent)]
    for c in range(1, CHUNKS):
        kernel = functools.partial(down_kernel, cuts[c], tile, count)
        shapes = kept_and_sent(rows, cuts[c : c + 1])
        produced.append(local_call(kernel, "down", shapes, [*rest, *downs]))
    return produced


def halved(block):
    half = block.shape[0] // 2
    return block[:half], block[half:].astype(jnp.bfloat16)


def ordered_after(value, earlier):
    return value if earlier is None else lax.optimization_barrier((value, earlier))[0]


def reduce_and_gather(halves, extra, routes):
    f32, bf16 = jnp.float32, jnp.bfloat16
    parts = [list(halves[2 * c : 2 * c + 2]) for c in range(CHUNKS)]
    for number, route in enumerate(routes.steps[:-1]):
        earlier = None
        for c, part in enumerate(parts):
            kept, sent = part
            kept = kept + ordered_after(exchange(sent, route), earlier).astype(f32)
            if number < len(routes.steps) - 2:
                part[:] = halved(kept)
            else:
                if c == CARRIER:
                    kept = jnp.concatenate([kept, extra.astype(f32)], axis=1)
                part[:] = kept, kept.astype(bf16)
            earlier = part[1]
    blocks, earlier = [], None
    for kept, sent in parts:
        half = kept.shape[0] // 2
        other = ordered_after(exchange(sent, routes.steps[-1]), earlier).astype(f32)
        blocks.append((kept + jnp.concatenate([other[half:], other[:half]], axis=0)).astype(bf16))
        earlier = blocks[-1]
    gathers = routes.steps[-2::-1] + routes.groups
    for route in gathers[:-1]:
        earlier = None
        for c, block in enumerate(blocks):
            other = ordered_after(exchange(block, route), earlier)
            blocks[c] = earlier = jnp.concatenate([block, other], axis=0)
    return [(block, exchange(block, gathers[-1])) for block in blocks]


def body(
    queries,
    tree_kv,
    kv_cache,
    block_table,
    cache_lengths,
    parents,
    w_out,
    w_gate,
    w_up,
    w_down,
    expert_ids,
    gate_weights,
):
    axis_width = lax.axis_size("wide")
    routes = Routes(axis_width)
    owners = (0, 1)
    own, fetched = attend(
        queries, tree_kv, kv_cache, block_table, cache_lengths, parents, w_out, expert_ids,
        gate_weights,
    )
    *halves, extra = project(own, exchange(own, routes.pair), fetched, expert_ids.shape[0])
    others = [exchange(x, routes.pair) for x in (w_gate, w_up, w_down)]
    feeds = [w_gate, w_up, *others[:2]]
    downs = [w_down, others[2]]
    hidden = reduce_and_gather(halves, extra, routes)
    parts = [list(pair) for pair in experts(hidden, owners, feeds, downs)]
    for route in routes.groups[::-1] + routes.returns[:-1]:
        earlier = None
        for part in parts:
            kept, sent = part
            other = ordered_after(exchange(sent, route), earlier)
            part[:] = halved(kept + other.astype(jnp.float32))
            earlier = part[1]
    results, earlier = [], None
    for kept, sent in parts:
        other = ordered_after(exchange(sent, routes.returns[-1]), earlier).astype(jnp.float32)
        results.append((kept + other).astype(jnp.bfloat16))
        earlier = results[-1]
    result = jnp.concatenate(results, axis=1)
    return jnp.where(on_odd_chip(), exchange(result, routes.pair), result)


def solution(mesh):
    placed = (
        P(("groups", "wide"), None),
        P(None, ("groups", "wide"), None),
        P(None, ("groups", "wide"), None, None),
        P(("groups", "wide"), None),
        P(("groups", "wide"), None),
        P(("groups", "wide"), None),
        P("wide", None),
        P("wide", None, None),
        P("wide", None, None),
        P("wide", None, None),
        P(("groups", "wide"), None),
        P(("groups", "wide"), None),
    )
    return jax.shard_map(
        body, mesh=mesh, in_specs=placed, out_specs=P(("groups", "wide"), None), check_vma=False
    )
```

```python
import functools

import jax
import jax.numpy as jnp
from jax import lax
from jax.experimental import pallas as pl
from jax.experimental.pallas import tpu as pltpu
from jax.sharding import PartitionSpec as P

ATT_TP = 8
PIECES = (8, 8)
CHUNKS = len(PIECES)
CARRIER = 0
LANES = 128
HINT = 30_000_000_000


def bits_of(count):
    return count.bit_length() - 1


def column_cuts(features):
    ends = [features * sum(PIECES[: c + 1]) // sum(PIECES) for c in range(CHUNKS)]
    return list(zip([0] + ends[:-1], ends))


def spare_width(axis_width):
    return -(-2 * axis_width // LANES) * LANES


def slice_orders(axis_width):
    low, *rest, high = [axis_width // ATT_TP << step for step in range(bits_of(ATT_TP))]
    return [*rest, high, low], [low, *rest, high]


def return_orders(axis_width):
    low, *rest, high = [axis_width // ATT_TP << step for step in range(bits_of(ATT_TP))]
    return [*rest, low, high], [low, high, *rest]


def exchange(block, route):
    count = lax.axis_size("wide")
    return lax.ppermute(block, "wide", [(i, route(i)) for i in range(count)])


def on_odd_chip():
    index = lax.axis_index("wide") // (lax.axis_size("wide") // ATT_TP)
    odd = 0
    for step in range(bits_of(ATT_TP)):
        odd ^= index >> step & 1
    return odd == 1


class Routes:
    def __init__(self, axis_width):
        groups = axis_width // ATT_TP
        orders = slice_orders(axis_width)
        odd = lambda i: (i // groups).bit_count() & 1
        self.pair = lambda i: i ^ 1
        steps = range(bits_of(ATT_TP))
        self.steps, self.returns = [
            [lambda i, order=order, k=k: i ^ order[(i & 1) ^ odd(i)][k] ^ 1 for k in steps]
            for order in (orders, return_orders(axis_width))
        ]
        self.groups = [lambda i, k=k: i ^ 1 << k for k in range(1, bits_of(groups))]


def relative_masks(order):
    steps = len(order)
    masks = []
    for j in range(1 << steps):
        mask = 0
        for step in range(steps):
            if j >> (steps - 1 - step) & 1:
                mask ^= order[step]
        masks.append(mask)
    return masks


def started(sources, targets, sems):
    copies = [
        pltpu.make_async_copy(source, target, sems.at[n])
        for n, (source, target) in enumerate(zip(sources, targets))
    ]
    for copy in copies:
        copy.start()
    return copies


def attend_kernel(axis_width, *refs):
    sources, (ordered, w_out), scratch = refs[:9], refs[9:11], refs[11:]
    *inputs, attended, sems = scratch
    *sources, pools, w_out_source = sources
    *others, pools_in = inputs
    sources = [*sources, pools.at[0], pools.at[1], w_out_source]
    copies = started(sources, [*others, pools_in.at[0], pools_in.at[1], w_out], sems)
    parents, table, lengths, expert_ids, gate_weights, queries, tree_kv, kv_cache = inputs
    seq_count, node_count = parents.shape
    head_dim = tree_kv.shape[-1]
    head_count = queries.shape[1] // head_dim
    pages = table.shape[1]
    cached = pages * kv_cache.shape[2]
    all_nodes = seq_count * node_count
    query_count = head_count * node_count
    f32, bf16 = jnp.float32, jnp.bfloat16

    copies[0].wait()
    lane = lax.broadcasted_iota(jnp.int32, (8, all_nodes), 1)
    shifted = [
        jnp.where(parents[s : s + 1, :] >= 0, parents[s : s + 1, :] + s * node_count, -1)
        for s in range(seq_count)
    ]
    above = jnp.broadcast_to(jnp.concatenate(shifted, axis=1), lane.shape)
    above = jnp.where(above >= 0, above, lane)
    words = jnp.left_shift(1, lane % node_count)
    for repeat in range(max(node_count - 1, 1).bit_length()):
        if repeat:
            above = jnp.take_along_axis(above, above, axis=1)
        words = words | jnp.take_along_axis(words, above, axis=1)

    for copy in copies[1:-2]:
        copy.wait()
    query_nodes = lax.broadcasted_iota(jnp.int32, (8, query_count), 1) % node_count
    node_rows = lax.broadcasted_iota(jnp.int32, (node_count, query_count), 0)
    positions = lax.broadcasted_iota(jnp.int32, (cached, query_count), 0)
    weighed = []
    for s in range(seq_count):
        own = slice(s * node_count, (s + 1) * node_count)
        word = jnp.take_along_axis(words, query_nodes + s * node_count, axis=1)
        word = jnp.broadcast_to(word[:1], node_rows.shape)
        tree_open = (lax.shift_right_logical(word, node_rows) & 1) == 1
        keys = [kv_cache[0, table[s, p]] for p in range(pages)]
        key_rows = jnp.concatenate(keys + [tree_kv[0, own]], axis=0)
        query_rows = jnp.concatenate(
            [queries[own, h * head_dim : (h + 1) * head_dim] for h in range(head_count)], axis=0
        )
        scores = lax.dot_general(
            key_rows, query_rows, (((1,), (1,)), ((), ())), preferred_element_type=f32
        ) * head_dim ** (-0.5)
        cache_scores = jnp.where(positions < lengths[0, s], scores[:cached], -jnp.inf)
        tree_scores = jnp.where(tree_open, scores[cached:], -jnp.inf)
        masked = jnp.concatenate([cache_scores, tree_scores], axis=0)
        highest = jnp.max(masked, axis=0, keepdims=True)
        probs = jnp.exp(masked - highest)
        total = jnp.broadcast_to(jnp.sum(probs, axis=0, keepdims=True), (head_dim, query_count))
        weighed.append((probs.astype(bf16), total))
    copies[-2].wait()
    for s, (probs, total) in enumerate(weighed):
        own = slice(s * node_count, (s + 1) * node_count)
        values = [kv_cache[1, table[s, p]] for p in range(pages)]
        value_rows = jnp.concatenate(values + [tree_kv[1, own]], axis=0)
        blended = lax.dot_general(
            probs, value_rows, (((0,), (0,)), ((), ())), preferred_element_type=f32
        )
        blended = (blended / total.T).astype(bf16)
        for h in range(head_count):
            attended[own, h * head_dim : (h + 1) * head_dim] = blended[
                h * node_count : (h + 1) * node_count
            ]

    listed, row_count = expert_ids.shape
    spread_width = spare_width(axis_width)
    expert = lax.broadcasted_iota(jnp.int32, (spread_width, row_count), 0)
    weight = jnp.zeros((spread_width, row_count), f32)
    for k in range(listed):
        weight += jnp.where(
            expert_ids[k : k + 1, :] == expert % axis_width, gate_weights[k : k + 1, :], 0.0
        )
    upper = weight.astype(bf16).astype(f32)
    parts = jnp.where(
        expert < axis_width, upper, jnp.where(expert < 2 * axis_width, weight - upper, 0.0)
    )
    ordered[:row_count, -spread_width:] = parts.T.astype(bf16)
    rest = (all_nodes - row_count, spread_width)
    ordered[row_count:, -spread_width:] = jnp.zeros(rest, bf16)

    device = lax.axis_index("wide")
    groups = axis_width // ATT_TP
    first, second = [relative_masks(order) for order in slice_orders(axis_width)]
    block = all_nodes // ATT_TP
    picked = []
    for one, other in zip(first, second):
        target = (device ^ jnp.where(device & 1 == 0, one, other)) // groups
        picked.append(attended[pl.ds(pl.multiple_of(target * block, block), block), :])
    ordered[:, : queries.shape[1]] = jnp.concatenate(picked, axis=0)
    copies[-1].wait()


def project_kernel(own_rows, cut, own, other, w_out, kept, sent, *extra):
    rows = jnp.where(on_odd_chip(), other[...], own[...])
    width = w_out.shape[0]
    if extra:
        extra[0][...] = rows[: 2 * own_rows, width:]
    half = rows.shape[0] // 2
    projected = jnp.dot(
        rows[:, :width], w_out[:, cut[0] : cut[1]], preferred_element_type=jnp.float32
    )
    kept[...] = projected[:half]
    sent[...] = projected[half:].astype(jnp.bfloat16)


def project(own, other, w_out, own_rows):
    spare = spare_width(lax.axis_size("wide"))
    halves = []
    for c, cut in enumerate(column_cuts(w_out.shape[1])):
        shapes = kept_and_sent(own.shape[0], [cut])
        last = c == CHUNKS - 1
        halves += local_call(
            functools.partial(project_kernel, own_rows, cut),
            "project",
            shapes + [pltpu.VMEM((2 * own_rows, spare), jnp.bfloat16)] * last,
            [own, other, w_out],
            flops=HINT * c,
        )
    return halves


def kept_and_sent(rows, cuts):
    shapes = []
    for low, high in cuts:
        shapes.append(pltpu.VMEM((rows // 2, high - low), jnp.float32))
        shapes.append(pltpu.VMEM((rows // 2, high - low), jnp.bfloat16))
    return shapes


def attend(
    queries, tree_kv, kv_cache, table, lengths, parents, w_out, expert_ids, gate_weights
):
    axis_width = lax.axis_size("wide")
    rows, width = queries.shape
    given = [parents, table, lengths, expert_ids.T, gate_weights.T, queries, tree_kv, kv_cache, w_out]
    spaces = [pltpu.VMEM, pltpu.SMEM, pltpu.SMEM] + [pltpu.VMEM] * 5
    given = [pltpu.with_memory_space_constraint(x, pltpu.HBM) for x in given]
    return pl.pallas_call(
        functools.partial(attend_kernel, axis_width),
        out_shape=[
            pltpu.VMEM((rows, width + spare_width(axis_width)), jnp.bfloat16),
            pltpu.VMEM(w_out.shape, w_out.dtype),
        ],
        in_specs=[pl.BlockSpec(memory_space=pltpu.HBM)] * len(given),
        out_specs=[pl.BlockSpec(memory_space=pltpu.VMEM)] * 2,
        scratch_shapes=[space(x.shape, x.dtype) for space, x in zip(spaces, given)]
        + [pltpu.VMEM(queries.shape, jnp.bfloat16), pltpu.SemaphoreType.DMA((len(given) + 1,))],
        compiler_params=pltpu.CompilerParams(vmem_limit_bytes=16 * 1024 * 1024),
        name="attend",
    )(*given)


def arranged(halves, columns, axis_width):
    rows = jnp.concatenate([half[:, columns] for half in halves], axis=0)
    groups = axis_width // ATT_TP
    block = rows.shape[0] // (groups // 2 * ATT_TP)
    results = []
    for order, other in zip(slice_orders(axis_width), return_orders(axis_width)):
        masks = relative_masks(order)
        places = [masks.index(mask) for mask in relative_masks(other)]
        starts = [(k * ATT_TP + place) * block for k in range(groups // 2) for place in places]
        results.append(jnp.concatenate([rows[x : x + block] for x in starts], axis=0))
    role = (lax.axis_index("wide") & 1) ^ on_odd_chip().astype(jnp.int32)
    return jnp.where(role == 0, results[0], results[1])


def feed_kernel(axis_width, cut, tile, pairs, first, *refs):
    hidden, weights, refs = refs[:2], refs[2 : 2 + pairs], refs[2 + pairs :]
    before, after = (None, refs) if first else (refs[:pairs], refs[pairs:])
    rows = arranged(hidden, slice(0, cut[1] - cut[0]), axis_width)
    for m in range(pairs):
        for n in range(weights[m].shape[2] // tile):
            columns = slice(n * tile, (n + 1) * tile)
            share = jnp.dot(
                rows, weights[m][0, cut[0] : cut[1], columns], preferred_element_type=jnp.float32
            )
            after[m][:, columns] = share if first else before[m][:, columns] + share


def finish_kernel(axis_width, spare, cut, out_cut, tile, owners, *refs):
    count = len(owners)
    hidden, carrier, refs = refs[:2], refs[2:4], refs[4:]
    feeds, downs, sums = refs[: 2 * count], refs[2 * count : 3 * count], refs[3 * count : 5 * count]
    kept, sent = refs[5 * count : 5 * count + 2]
    activated, row_weight = refs[5 * count + 2 : 6 * count + 2], refs[6 * count + 2 :]
    f32, bf16 = jnp.float32, jnp.bfloat16
    width = cut[1] - cut[0]
    device = lax.axis_index("wide")
    rows = arranged(hidden, slice(0, width), axis_width)
    parts = arranged(carrier, slice(-spare, None), axis_width)
    lane = lax.broadcasted_iota(jnp.int32, parts.shape, 1)
    piece = slice(*cut)
    for m, owner in enumerate(owners):
        expert = device ^ owner
        mine = (lane == expert) | (lane == expert + axis_width)
        row_weight[m][...] = jnp.sum(jnp.where(mine, parts.astype(f32), 0.0), axis=1, keepdims=True)
        for n in range(feeds[2 * m].shape[2] // tile):
            columns = slice(n * tile, (n + 1) * tile)
            gate_part, up_part = [
                sums[2 * m + k][:, columns]
                + jnp.dot(rows, feeds[2 * m + k][0, piece, columns], preferred_element_type=f32)
                for k in range(2)
            ]
            activated[m][:, columns] = (
                gate_part / (1.0 + jnp.exp(-gate_part)) * up_part
            ).astype(bf16)
    produce(activated, downs, row_weight, out_cut, kept, sent, tile)


def down_kernel(cut, tile, count, *refs):
    activated, row_weight, downs = [refs[k * count : (k + 1) * count] for k in range(3)]
    produce(activated, downs, row_weight, cut, *refs[3 * count :], tile)


def produce(activated, downs, row_weight, cut, kept, sent, tile):
    half, width = kept.shape
    for start in range(0, width, tile):
        size = min(tile, width - start)
        columns = slice(cut[0] + start, cut[0] + start + size)
        weighted = 0.0
        for rows, w_down, weight in zip(activated, downs, row_weight):
            weighted += (
                jnp.dot(rows[...], w_down[0, :, columns], preferred_element_type=jnp.float32)
                * weight[...]
            )
        kept[:, start : start + size] = weighted[:half]
        sent[:, start : start + size] = weighted[half:].astype(jnp.bfloat16)


def local_call(kernel, name, out_shape, given, flops=0):
    return pl.pallas_call(
        kernel,
        out_shape=out_shape,
        in_specs=[pl.BlockSpec(memory_space=pltpu.VMEM)] * len(given),
        out_specs=[pl.BlockSpec(memory_space=pltpu.VMEM)] * len(out_shape),
        compiler_params=pltpu.CompilerParams(vmem_limit_bytes=16 * 1024 * 1024),
        cost_estimate=pl.CostEstimate(flops=flops, bytes_accessed=0, transcendentals=0) if flops else None,
        name=name,
    )(*given)


def experts(hidden, owners, feeds, downs):
    axis_width = lax.axis_size("wide")
    rows = 2 * hidden[0][0].shape[0]
    hidden_width, features = downs[0].shape[1:]
    cuts = column_cuts(features)
    spare = spare_width(axis_width)
    count = len(owners)
    tile = 256 if hidden_width % 256 == 0 else LANES
    wide = pltpu.VMEM((rows, hidden_width), jnp.float32)
    sums = []
    for c in range(CHUNKS - 1):
        kernel = functools.partial(feed_kernel, axis_width, cuts[c], tile, 2 * count, c == 0)
        sums = local_call(kernel, "feed", [wide] * (2 * count), [*hidden[c], *feeds, *sums])
    kept, sent, *rest = local_call(
        functools.partial(finish_kernel, axis_width, spare, cuts[-1], cuts[0], tile, owners),
        "finish",
        kept_and_sent(rows, cuts[:1])
        + [pltpu.VMEM((rows, hidden_width), jnp.bfloat16)] * count
        + [pltpu.VMEM((rows, 1), jnp.float32)] * count,
        [*hidden[-1], *hidden[CARRIER], *feeds, *downs, *sums],
    )
    produced = [(kept, sent)]
    for c in range(1, CHUNKS):
        kernel = functools.partial(down_kernel, cuts[c], tile, count)
        shapes = kept_and_sent(rows, cuts[c : c + 1])
        produced.append(local_call(kernel, "down", shapes, [*rest, *downs]))
    return produced


def halved(block):
    half = block.shape[0] // 2
    return block[:half], block[half:].astype(jnp.bfloat16)


def ordered_after(value, earlier):
    return value if earlier is None else lax.optimization_barrier((value, earlier))[0]


def reduce_and_gather(halves, extra, routes):
    f32, bf16 = jnp.float32, jnp.bfloat16
    parts = [list(halves[2 * c : 2 * c + 2]) for c in range(CHUNKS)]
    for number, route in enumerate(routes.steps[:-1]):
        earlier = None
        for c, part in enumerate(parts):
            kept, sent = part
            kept = kept + ordered_after(exchange(sent, route), earlier).astype(f32)
            if number < len(routes.steps) - 2:
                part[:] = halved(kept)
            else:
                if c == CARRIER:
                    kept = jnp.concatenate([kept, extra.astype(f32)], axis=1)
                part[:] = kept, kept.astype(bf16)
            earlier = part[1]
    blocks, earlier = [], None
    for kept, sent in parts:
        half = kept.shape[0] // 2
        other = ordered_after(exchange(sent, routes.steps[-1]), earlier).astype(f32)
        blocks.append((kept + jnp.concatenate([other[half:], other[:half]], axis=0)).astype(bf16))
        earlier = blocks[-1]
    gathers = routes.steps[-2::-1] + routes.groups
    for route in gathers[:-1]:
        earlier = None
        for c, block in enumerate(blocks):
            other = ordered_after(exchange(block, route), earlier)
            blocks[c] = earlier = jnp.concatenate([block, other], axis=0)
    return [(block, exchange(block, gathers[-1])) for block in blocks]


def body(
    queries,
    tree_kv,
    kv_cache,
    block_table,
    cache_lengths,
    parents,
    w_out,
    w_gate,
    w_up,
    w_down,
    expert_ids,
    gate_weights,
):
    axis_width = lax.axis_size("wide")
    routes = Routes(axis_width)
    owners = (0, 1)
    own, fetched = attend(
        queries, tree_kv, kv_cache, block_table, cache_lengths, parents, w_out, expert_ids,
        gate_weights,
    )
    *halves, extra = project(own, exchange(own, routes.pair), fetched, expert_ids.shape[0])
    others = [exchange(x, routes.pair) for x in (w_gate, w_up, w_down)]
    feeds = [w_gate, w_up, *others[:2]]
    downs = [w_down, others[2]]
    hidden = reduce_and_gather(halves, extra, routes)
    parts = [list(pair) for pair in experts(hidden, owners, feeds, downs)]
    for route in routes.groups[::-1] + routes.returns[:-1]:
        earlier = None
        for part in parts:
            kept, sent = part
            other = ordered_after(exchange(sent, route), earlier)
            part[:] = halved(kept + other.astype(jnp.float32))
            earlier = part[1]
    results, earlier = [], None
    for kept, sent in parts:
        other = ordered_after(exchange(sent, routes.returns[-1]), earlier).astype(jnp.float32)
        results.append((kept + other).astype(jnp.bfloat16))
        earlier = results[-1]
    result = jnp.concatenate(results, axis=1)
    return jnp.where(on_odd_chip(), exchange(result, routes.pair), result)


def solution(mesh):
    placed = (
        P(("groups", "wide"), None),
        P(None, ("groups", "wide"), None),
        P(None, ("groups", "wide"), None, None),
        P(("groups", "wide"), None),
        P(("groups", "wide"), None),
        P(("groups", "wide"), None),
        P("wide", None),
        P("wide", None, None),
        P("wide", None, None),
        P("wide", None, None),
        P(("groups", "wide"), None),
        P(("groups", "wide"), None),
    )
    return jax.shard_map(
        body, mesh=mesh, in_specs=placed, out_specs=P(("groups", "wide"), None), check_vma=False
    )
```

```python
import functools

import jax
import jax.numpy as jnp
from jax import lax
from jax.experimental import pallas as pl
from jax.experimental.pallas import tpu as pltpu
from jax.sharding import PartitionSpec as P

ATT_TP = 8
PIECES = (8, 8)
CHUNKS = len(PIECES)
CARRIER = 0
LANES = 128
HINT = 30_000_000_000


def bits_of(count):
    return count.bit_length() - 1


def column_cuts(features):
    ends = [features * sum(PIECES[: c + 1]) // sum(PIECES) for c in range(CHUNKS)]
    return list(zip([0] + ends[:-1], ends))


def spare_width(axis_width):
    return -(-2 * axis_width // LANES) * LANES


def slice_orders(axis_width):
    low, *rest, high = [axis_width // ATT_TP << step for step in range(bits_of(ATT_TP))]
    return [*rest, high, low], [low, *rest, high]


def return_orders(axis_width):
    low, *rest, high = [axis_width // ATT_TP << step for step in range(bits_of(ATT_TP))]
    return [*rest, low, high], [low, high, *rest]


def exchange(block, route):
    count = lax.axis_size("wide")
    return lax.ppermute(block, "wide", [(i, route(i)) for i in range(count)])


def on_odd_chip():
    index = lax.axis_index("wide") // (lax.axis_size("wide") // ATT_TP)
    odd = 0
    for step in range(bits_of(ATT_TP)):
        odd ^= index >> step & 1
    return odd == 1


class Routes:
    def __init__(self, axis_width):
        groups = axis_width // ATT_TP
        orders = slice_orders(axis_width)
        odd = lambda i: (i // groups).bit_count() & 1
        self.pair = lambda i: i ^ 1
        steps = range(bits_of(ATT_TP))
        self.steps, self.returns = [
            [lambda i, order=order, k=k: i ^ order[(i & 1) ^ odd(i)][k] ^ 1 for k in steps]
            for order in (orders, return_orders(axis_width))
        ]
        self.groups = [lambda i, k=k: i ^ 1 << k for k in range(1, bits_of(groups))]


def relative_masks(order):
    steps = len(order)
    masks = []
    for j in range(1 << steps):
        mask = 0
        for step in range(steps):
            if j >> (steps - 1 - step) & 1:
                mask ^= order[step]
        masks.append(mask)
    return masks


def started(sources, targets, sems):
    copies = [
        pltpu.make_async_copy(source, target, sems.at[n])
        for n, (source, target) in enumerate(zip(sources, targets))
    ]
    for copy in copies:
        copy.start()
    return copies


def attend_kernel(axis_width, *refs):
    sources, (ordered, w_out), scratch = refs[:9], refs[9:11], refs[11:]
    *inputs, attended, sems = scratch
    *sources, pools, w_out_source = sources
    *others, pools_in = inputs
    sources = [*sources, pools.at[0], pools.at[1], w_out_source]
    copies = started(sources, [*others, pools_in.at[0], pools_in.at[1], w_out], sems)
    parents, table, lengths, expert_ids, gate_weights, queries, tree_kv, kv_cache = inputs
    seq_count, node_count = parents.shape
    head_dim = tree_kv.shape[-1]
    head_count = queries.shape[1] // head_dim
    pages = table.shape[1]
    cached = pages * kv_cache.shape[2]
    all_nodes = seq_count * node_count
    query_count = head_count * node_count
    f32, bf16 = jnp.float32, jnp.bfloat16

    copies[0].wait()
    lane = lax.broadcasted_iota(jnp.int32, (8, all_nodes), 1)
    shifted = [
        jnp.where(parents[s : s + 1, :] >= 0, parents[s : s + 1, :] + s * node_count, -1)
        for s in range(seq_count)
    ]
    above = jnp.broadcast_to(jnp.concatenate(shifted, axis=1), lane.shape)
    above = jnp.where(above >= 0, above, lane)
    words = jnp.left_shift(1, lane % node_count)
    for repeat in range(max(node_count - 1, 1).bit_length()):
        if repeat:
            above = jnp.take_along_axis(above, above, axis=1)
        words = words | jnp.take_along_axis(words, above, axis=1)

    for copy in copies[1:-2]:
        copy.wait()
    query_nodes = lax.broadcasted_iota(jnp.int32, (8, query_count), 1) % node_count
    node_rows = lax.broadcasted_iota(jnp.int32, (node_count, query_count), 0)
    positions = lax.broadcasted_iota(jnp.int32, (cached, query_count), 0)
    weighed = []
    for s in range(seq_count):
        own = slice(s * node_count, (s + 1) * node_count)
        word = jnp.take_along_axis(words, query_nodes + s * node_count, axis=1)
        word = jnp.broadcast_to(word[:1], node_rows.shape)
        tree_open = (lax.shift_right_logical(word, node_rows) & 1) == 1
        keys = [kv_cache[0, table[s, p]] for p in range(pages)]
        key_rows = jnp.concatenate(keys + [tree_kv[0, own]], axis=0)
        query_rows = jnp.concatenate(
            [queries[own, h * head_dim : (h + 1) * head_dim] for h in range(head_count)], axis=0
        )
        scores = lax.dot_general(
            key_rows, query_rows, (((1,), (1,)), ((), ())), preferred_element_type=f32
        ) * head_dim ** (-0.5)
        cache_scores = jnp.where(positions < lengths[0, s], scores[:cached], -jnp.inf)
        tree_scores = jnp.where(tree_open, scores[cached:], -jnp.inf)
        masked = jnp.concatenate([cache_scores, tree_scores], axis=0)
        highest = jnp.max(masked, axis=0, keepdims=True)
        probs = jnp.exp(masked - highest)
        total = jnp.broadcast_to(jnp.sum(probs, axis=0, keepdims=True), (head_dim, query_count))
        weighed.append((probs.astype(bf16), total))
    copies[-2].wait()
    for s, (probs, total) in enumerate(weighed):
        own = slice(s * node_count, (s + 1) * node_count)
        values = [kv_cache[1, table[s, p]] for p in range(pages)]
        value_rows = jnp.concatenate(values + [tree_kv[1, own]], axis=0)
        blended = lax.dot_general(
            probs, value_rows, (((0,), (0,)), ((), ())), preferred_element_type=f32
        )
        blended = (blended / total.T).astype(bf16)
        for h in range(head_count):
            attended[own, h * head_dim : (h + 1) * head_dim] = blended[
                h * node_count : (h + 1) * node_count
            ]

    listed, row_count = expert_ids.shape
    spread_width = spare_width(axis_width)
    expert = lax.broadcasted_iota(jnp.int32, (spread_width, row_count), 0)
    weight = jnp.zeros((spread_width, row_count), f32)
    for k in range(listed):
        weight += jnp.where(
            expert_ids[k : k + 1, :] == expert % axis_width, gate_weights[k : k + 1, :], 0.0
        )
    upper = weight.astype(bf16).astype(f32)
    parts = jnp.where(
        expert < axis_width, upper, jnp.where(expert < 2 * axis_width, weight - upper, 0.0)
    )
    ordered[:row_count, -spread_width:] = parts.T.astype(bf16)
    rest = (all_nodes - row_count, spread_width)
    ordered[row_count:, -spread_width:] = jnp.zeros(rest, bf16)

    device = lax.axis_index("wide")
    groups = axis_width // ATT_TP
    first, second = [relative_masks(order) for order in slice_orders(axis_width)]
    block = all_nodes // ATT_TP
    picked = []
    for one, other in zip(first, second):
        target = (device ^ jnp.where(device & 1 == 0, one, other)) // groups
        picked.append(attended[pl.ds(pl.multiple_of(target * block, block), block), :])
    ordered[:, : queries.shape[1]] = jnp.concatenate(picked, axis=0)
    copies[-1].wait()


def project_kernel(own_rows, cut, own, other, w_out, kept, sent, *extra):
    rows = jnp.where(on_odd_chip(), other[...], own[...])
    width = w_out.shape[0]
    if extra:
        extra[0][...] = rows[: 2 * own_rows, width:]
    half = rows.shape[0] // 2
    projected = jnp.dot(
        rows[:, :width], w_out[:, cut[0] : cut[1]], preferred_element_type=jnp.float32
    )
    kept[...] = projected[:half]
    sent[...] = projected[half:].astype(jnp.bfloat16)


def project(own, other, w_out, own_rows):
    spare = spare_width(lax.axis_size("wide"))
    halves = []
    for c, cut in enumerate(column_cuts(w_out.shape[1])):
        shapes = kept_and_sent(own.shape[0], [cut])
        last = c == CHUNKS - 1
        halves += local_call(
            functools.partial(project_kernel, own_rows, cut),
            "project",
            shapes + [pltpu.VMEM((2 * own_rows, spare), jnp.bfloat16)] * last,
            [own, other, w_out],
            flops=HINT * c,
        )
    return halves


def kept_and_sent(rows, cuts):
    shapes = []
    for low, high in cuts:
        shapes.append(pltpu.VMEM((rows // 2, high - low), jnp.float32))
        shapes.append(pltpu.VMEM((rows // 2, high - low), jnp.bfloat16))
    return shapes


def attend(
    queries, tree_kv, kv_cache, table, lengths, parents, w_out, expert_ids, gate_weights
):
    axis_width = lax.axis_size("wide")
    rows, width = queries.shape
    given = [parents, table, lengths, expert_ids.T, gate_weights.T, queries, tree_kv, kv_cache, w_out]
    spaces = [pltpu.VMEM, pltpu.SMEM, pltpu.SMEM] + [pltpu.VMEM] * 5
    given = [pltpu.with_memory_space_constraint(x, pltpu.HBM) for x in given]
    return pl.pallas_call(
        functools.partial(attend_kernel, axis_width),
        out_shape=[
            pltpu.VMEM((rows, width + spare_width(axis_width)), jnp.bfloat16),
            pltpu.VMEM(w_out.shape, w_out.dtype),
        ],
        in_specs=[pl.BlockSpec(memory_space=pltpu.HBM)] * len(given),
        out_specs=[pl.BlockSpec(memory_space=pltpu.VMEM)] * 2,
        scratch_shapes=[space(x.shape, x.dtype) for space, x in zip(spaces, given)]
        + [pltpu.VMEM(queries.shape, jnp.bfloat16), pltpu.SemaphoreType.DMA((len(given) + 1,))],
        compiler_params=pltpu.CompilerParams(vmem_limit_bytes=16 * 1024 * 1024),
        name="attend",
    )(*given)


def arranged(halves, columns, axis_width):
    rows = jnp.concatenate([half[:, columns] for half in halves], axis=0)
    groups = axis_width // ATT_TP
    block = rows.shape[0] // (groups // 2 * ATT_TP)
    results = []
    for order, other in zip(slice_orders(axis_width), return_orders(axis_width)):
        masks = relative_masks(order)
        places = [masks.index(mask) for mask in relative_masks(other)]
        starts = [(k * ATT_TP + place) * block for k in range(groups // 2) for place in places]
        results.append(jnp.concatenate([rows[x : x + block] for x in starts], axis=0))
    role = (lax.axis_index("wide") & 1) ^ on_odd_chip().astype(jnp.int32)
    return jnp.where(role == 0, results[0], results[1])


def feed_kernel(axis_width, cut, tile, pairs, first, *refs):
    hidden, weights, refs = refs[:2], refs[2 : 2 + pairs], refs[2 + pairs :]
    before, after = (None, refs) if first else (refs[:pairs], refs[pairs:])
    rows = arranged(hidden, slice(0, cut[1] - cut[0]), axis_width)
    for m in range(pairs):
        for n in range(weights[m].shape[2] // tile):
            columns = slice(n * tile, (n + 1) * tile)
            share = jnp.dot(
                rows, weights[m][0, cut[0] : cut[1], columns], preferred_element_type=jnp.float32
            )
            after[m][:, columns] = share if first else before[m][:, columns] + share


def finish_kernel(axis_width, spare, cut, out_cut, tile, owners, *refs):
    count = len(owners)
    hidden, carrier, refs = refs[:2], refs[2:4], refs[4:]
    feeds, downs, sums = refs[: 2 * count], refs[2 * count : 3 * count], refs[3 * count : 5 * count]
    kept, sent = refs[5 * count : 5 * count + 2]
    activated, row_weight = refs[5 * count + 2 : 6 * count + 2], refs[6 * count + 2 :]
    f32, bf16 = jnp.float32, jnp.bfloat16
    width = cut[1] - cut[0]
    device = lax.axis_index("wide")
    rows = arranged(hidden, slice(0, width), axis_width)
    parts = arranged(carrier, slice(-spare, None), axis_width)
    lane = lax.broadcasted_iota(jnp.int32, parts.shape, 1)
    piece = slice(*cut)
    for m, owner in enumerate(owners):
        expert = device ^ owner
        mine = (lane == expert) | (lane == expert + axis_width)
        row_weight[m][...] = jnp.sum(jnp.where(mine, parts.astype(f32), 0.0), axis=1, keepdims=True)
        for n in range(feeds[2 * m].shape[2] // tile):
            columns = slice(n * tile, (n + 1) * tile)
            gate_part, up_part = [
                sums[2 * m + k][:, columns]
                + jnp.dot(rows, feeds[2 * m + k][0, piece, columns], preferred_element_type=f32)
                for k in range(2)
            ]
            activated[m][:, columns] = (
                gate_part / (1.0 + jnp.exp(-gate_part)) * up_part
            ).astype(bf16)
    produce(activated, downs, row_weight, out_cut, kept, sent, tile)


def down_kernel(cut, tile, count, *refs):
    activated, row_weight, downs = [refs[k * count : (k + 1) * count] for k in range(3)]
    produce(activated, downs, row_weight, cut, *refs[3 * count :], tile)


def produce(activated, downs, row_weight, cut, kept, sent, tile):
    half, width = kept.shape
    for start in range(0, width, tile):
        size = min(tile, width - start)
        columns = slice(cut[0] + start, cut[0] + start + size)
        weighted = 0.0
        for rows, w_down, weight in zip(activated, downs, row_weight):
            weighted += (
                jnp.dot(rows[...], w_down[0, :, columns], preferred_element_type=jnp.float32)
                * weight[...]
            )
        kept[:, start : start + size] = weighted[:half]
        sent[:, start : start + size] = weighted[half:].astype(jnp.bfloat16)


def local_call(kernel, name, out_shape, given, flops=0):
    return pl.pallas_call(
        kernel,
        out_shape=out_shape,
        in_specs=[pl.BlockSpec(memory_space=pltpu.VMEM)] * len(given),
        out_specs=[pl.BlockSpec(memory_space=pltpu.VMEM)] * len(out_shape),
        compiler_params=pltpu.CompilerParams(vmem_limit_bytes=16 * 1024 * 1024),
        cost_estimate=pl.CostEstimate(flops=flops, bytes_accessed=0, transcendentals=0) if flops else None,
        name=name,
    )(*given)


def experts(hidden, owners, feeds, downs):
    axis_width = lax.axis_size("wide")
    rows = 2 * hidden[0][0].shape[0]
    hidden_width, features = downs[0].shape[1:]
    cuts = column_cuts(features)
    spare = spare_width(axis_width)
    count = len(owners)
    tile = 256 if hidden_width % 256 == 0 else LANES
    wide = pltpu.VMEM((rows, hidden_width), jnp.float32)
    sums = []
    for c in range(CHUNKS - 1):
        kernel = functools.partial(feed_kernel, axis_width, cuts[c], tile, 2 * count, c == 0)
        sums = local_call(kernel, "feed", [wide] * (2 * count), [*hidden[c], *feeds, *sums])
    kept, sent, *rest = local_call(
        functools.partial(finish_kernel, axis_width, spare, cuts[-1], cuts[0], tile, owners),
        "finish",
        kept_and_sent(rows, cuts[:1])
        + [pltpu.VMEM((rows, hidden_width), jnp.bfloat16)] * count
        + [pltpu.VMEM((rows, 1), jnp.float32)] * count,
        [*hidden[-1], *hidden[CARRIER], *feeds, *downs, *sums],
    )
    produced = [(kept, sent)]
    for c in range(1, CHUNKS):
        kernel = functools.partial(down_kernel, cuts[c], tile, count)
        shapes = kept_and_sent(rows, cuts[c : c + 1])
        produced.append(local_call(kernel, "down", shapes, [*rest, *downs]))
    return produced


def halved(block):
    half = block.shape[0] // 2
    return block[:half], block[half:].astype(jnp.bfloat16)


def ordered_after(value, earlier):
    return value if earlier is None else lax.optimization_barrier((value, earlier))[0]


def reduce_and_gather(halves, extra, routes):
    f32, bf16 = jnp.float32, jnp.bfloat16
    parts = [list(halves[2 * c : 2 * c + 2]) for c in range(CHUNKS)]
    for number, route in enumerate(routes.steps[:-1]):
        earlier = None
        for c, part in enumerate(parts):
            kept, sent = part
            kept = kept + ordered_after(exchange(sent, route), earlier).astype(f32)
            if number < len(routes.steps) - 2:
                part[:] = halved(kept)
            else:
                if c == CARRIER:
                    kept = jnp.concatenate([kept, extra.astype(f32)], axis=1)
                part[:] = kept, kept.astype(bf16)
            earlier = part[1]
    blocks, earlier = [], None
    for kept, sent in parts:
        half = kept.shape[0] // 2
        other = ordered_after(exchange(sent, routes.steps[-1]), earlier).astype(f32)
        blocks.append((kept + jnp.concatenate([other[half:], other[:half]], axis=0)).astype(bf16))
        earlier = blocks[-1]
    gathers = routes.steps[-2::-1] + routes.groups
    for route in gathers[:-1]:
        earlier = None
        for c, block in enumerate(blocks):
            other = ordered_after(exchange(block, route), earlier)
            blocks[c] = earlier = jnp.concatenate([block, other], axis=0)
    return [(block, exchange(block, gathers[-1])) for block in blocks]


def body(
    queries,
    tree_kv,
    kv_cache,
    block_table,
    cache_lengths,
    parents,
    w_out,
    w_gate,
    w_up,
    w_down,
    expert_ids,
    gate_weights,
):
    axis_width = lax.axis_size("wide")
    routes = Routes(axis_width)
    owners = (0, 1)
    own, fetched = attend(
        queries, tree_kv, kv_cache, block_table, cache_lengths, parents, w_out, expert_ids,
        gate_weights,
    )
    *halves, extra = project(own, exchange(own, routes.pair), fetched, expert_ids.shape[0])
    others = [exchange(x, routes.pair) for x in (w_gate, w_up, w_down)]
    feeds = [w_gate, w_up, *others[:2]]
    downs = [w_down, others[2]]
    hidden = reduce_and_gather(halves, extra, routes)
    parts = [list(pair) for pair in experts(hidden, owners, feeds, downs)]
    for route in routes.groups[::-1] + routes.returns[:-1]:
        earlier = None
        for part in parts:
            kept, sent = part
            other = ordered_after(exchange(sent, route), earlier)
            part[:] = halved(kept + other.astype(jnp.float32))
            earlier = part[1]
    results = []
    for kept, sent in parts:
        other = exchange(sent, routes.returns[-1]).astype(jnp.float32)
        results.append((kept + other).astype(jnp.bfloat16))
    result = jnp.concatenate(results, axis=1)
    return jnp.where(on_odd_chip(), exchange(result, routes.pair), result)


def solution(mesh):
    placed = (
        P(("groups", "wide"), None),
        P(None, ("groups", "wide"), None),
        P(None, ("groups", "wide"), None, None),
        P(("groups", "wide"), None),
        P(("groups", "wide"), None),
        P(("groups", "wide"), None),
        P("wide", None),
        P("wide", None, None),
        P("wide", None, None),
        P("wide", None, None),
        P(("groups", "wide"), None),
        P(("groups", "wide"), None),
    )
    return jax.shard_map(
        body, mesh=mesh, in_specs=placed, out_specs=P(("groups", "wide"), None), check_vma=False
    )
```
